128 devices in a mesh: dp: 8 (over z, x_hi), mp: 16 (over x_lo, y, core).
Axes of the slice: x: 4 (x_hi: 2, x_lo: 2; x = x_hi * 2 + x_lo), y: 4, z: 4, core: 2. Of those that a mesh axis runs over, the one named last changes fastest.
Arguments:
- hidden_in: bfloat16 [16384, 8192], P('dp', 'mp'), may hold values from -6 to 6
- positions: int32 [16384], P('dp'), may hold values from 0 to 127, as said below
- assignment: int32 [8, 16], P('dp'), may hold values from 0 to 15, each once within a row
- query_weight: bfloat16 [8192, 8192], P(None, 'mp'), may hold values from -0.0625 to 0.0625
- kv_weight: bfloat16 [8192, 2048], P(None, 'mp'), may hold values from -0.0625 to 0.0625
- dt_weight: float32 [8192, 64], replicated, may hold values from -0.0625 to 0.0625
- dt_bias: float32 [64], replicated, may hold values from -3 to -1
- decay_log: float32 [64], replicated, may hold values from -5.3 to -0.7
- skip_gain: float32 [64], replicated, may hold values from 0.5 to 1.5
Outputs:
- student_out: bfloat16 [16384, 8192], P(('dp', 'mp'))
- grad_dt_weight: float32 [8192, 64], replicated
- grad_dt_bias: float32 [64], replicated
- grad_decay_log: float32 [64], replicated
- grad_skip_gain: float32 [64], replicated
- loss: float32 [], replicated
The draws below stay inside these ranges and needn't reach their ends.
Inputs may be any that keep to these rules, and one draw needn't show every extreme that they name: `assignment`: row g lists each of the 16 sequences of group g once. positions count up by one from 0 at each document start; every sequence of 128 rows begins a document, and the first sequence is one whole document.
All inputs are finite; a program needn't handle non-finite values.
Results may differ from the reference program's by a relative error of at most 0.0065.
Values may be sent and summed in bfloat16 or wider, within the bound.
A program may use at most 128 MiB of HBM per device.

```python
import jax
import jax.numpy as jnp
from jax import lax

D = 8192
QH = 64
KVH = 8
HD = 128
L = 128
GROUPS = 8
GROUP_SEQS = 16
SEQS = 128
TOKENS = 16384


def draw_hidden_in(key, part):
    key = jax.random.fold_in(key, 5)
    first = jax.random.fold_in(key, 0)
    values = jnp.clip(jax.random.normal(first, (TOKENS, D), jnp.float32), -5.5, 5.5)
    return values.astype(jnp.bfloat16)


def draw_positions(key, part):
    key = jax.random.fold_in(key, 11)
    index = jnp.arange(TOKENS, dtype=jnp.int32)
    random_starts = (jax.random.randint(key, (TOKENS,), 0, 24) == 0) & (index >= L)
    starts = random_starts | (index % L == 0)
    marked = jnp.where(starts, index, 0)
    return index - lax.cummax(marked, axis=0)


def steps_of(own_key, dims, shards, low, largest):
    factor_of, own = 1.0, jax.random.fold_in(own_key, 6)
    for dim, parts in shards:
        draws = jnp.exp(jax.random.uniform(jax.random.fold_in(own, dim), (parts,), jnp.float32, low / len(shards), largest / len(shards)))
        factor_of = factor_of * jnp.repeat(draws, dims[dim] // parts).reshape([-1 if axis == dim else 1 for axis in range(len(dims))])
    return factor_of


def bell_draw(rng, dims, deviation, reach, shards=(), kind=jnp.bfloat16):
    result = jax.random.normal(rng, dims, jnp.float32) * deviation
    if len(shards) > 0:
        result = steps_of(rng, dims, shards, -0.22, 0.18) * result
    return jnp.clip(result, min=-reach, max=reach).astype(kind)


def setup_inputs(seed: int = 0) -> dict:
    keys = jax.random.split(jax.random.key(seed), 10)
    hidden_in = draw_hidden_in(jax.random.fold_in(keys[9], 71), 0)
    positions = draw_positions(jax.random.fold_in(keys[9], 71), 0)
    assignment = jax.vmap(lambda own: jax.random.permutation(own, GROUP_SEQS))(jax.random.split(keys[2], GROUPS)).reshape((GROUPS, GROUP_SEQS)).astype(jnp.int32)
    query_weight = bell_draw(keys[3], (D, QH * HD), D ** -0.5, 0.0625, ((1, 16),))
    kv_weight = bell_draw(keys[4], (D, 2 * KVH * HD), D ** -0.5, 0.0625, ((1, 16),))
    dt_weight = bell_draw(keys[5], (D, QH), D ** -0.5, 0.0625, (), jnp.float32)
    dt_bias = jnp.clip(jax.random.uniform(keys[6], (QH,), jnp.float32, -3.0, -1.0), -3.0, -1.0)
    decay_log = jnp.clip(jax.random.uniform(keys[7], (QH,), jnp.float32, -5.3, -0.7), -5.3, -0.7)
    skip_gain = jnp.clip(jax.random.uniform(keys[8], (QH,), jnp.float32, 0.5, 1.5), 0.5, 1.5)
    return {"hidden_in": hidden_in, "positions": positions, "assignment": assignment, "query_weight": query_weight, "kv_weight": kv_weight, "dt_weight": dt_weight, "dt_bias": dt_bias, "decay_log": decay_log, "skip_gain": skip_gain}


highest = lax.Precision.HIGHEST

def rotate(values, spots):
    half = HD // 2
    frequency = 500000.0 ** (-jnp.arange(half, dtype=jnp.float32) * 2.0 / HD)
    angle = spots.astype(jnp.float32)[:, None] * frequency[None, :]
    cosine = jnp.cos(angle)[:, None, :]
    sine = jnp.sin(angle)[:, None, :]
    first = values[..., :half].astype(jnp.float32)
    second = values[..., half:].astype(jnp.float32)
    turned = jnp.concatenate([first * cosine - second * sine, second * cosine + first * sine], axis=-1)
    return turned.astype(jnp.bfloat16)

def teacher_group(rows, spots, query_weight, kv_weight):
    count = rows.shape[0]
    seqs = count // L
    ratio = QH // KVH
    query = jnp.dot(rows, query_weight, preferred_element_type=jnp.float32).astype(jnp.bfloat16)
    key_value = jnp.dot(rows, kv_weight, preferred_element_type=jnp.float32).astype(jnp.bfloat16)
    query_turned = rotate(query.reshape(count, QH, HD), spots).reshape(seqs, L, KVH, ratio, HD)
    pairs = key_value.reshape(count, KVH, 2, HD)
    key_turned = rotate(pairs[:, :, 0], spots).reshape(seqs, L, KVH, HD)
    values = pairs[:, :, 1].reshape(seqs, L, KVH, HD)
    scores = jnp.einsum('slgjd,smgd->sgjlm', query_turned.astype(jnp.float32), key_turned.astype(jnp.float32), precision=highest) * HD ** (-0.5)
    causal = jnp.tril(jnp.ones((L, L), bool))
    scores = jnp.where(causal, scores, -jnp.inf)
    biggest = lax.optimization_barrier(jnp.max(scores, axis=-1, keepdims=True))
    weights = jnp.exp(scores - biggest)
    probabilities = (weights / lax.optimization_barrier(jnp.sum(weights, axis=-1, keepdims=True))).astype(jnp.bfloat16)
    target = jnp.einsum('sgjlm,smgd->slgjd', probabilities.astype(jnp.float32), values.astype(jnp.float32), precision=highest)
    return (query, key_value, target.astype(jnp.bfloat16).reshape(count, QH * HD))

def student(dt_weight, dt_bias, decay_log, skip_gain, rows, query, key_value):
    seq_len = rows.shape[0]
    ratio = QH // KVH
    step_size = jax.nn.softplus(jnp.dot(rows.astype(jnp.float32), dt_weight, precision=highest) + dt_bias)
    level = jnp.cumsum(step_size * -jnp.exp(decay_log), axis=0)
    level = level.T.reshape(KVH, ratio, seq_len)
    widths = step_size.T.reshape(KVH, ratio, 1, seq_len)
    query_wide = query.astype(jnp.float32).reshape(seq_len, KVH, ratio, HD)
    pairs = key_value.astype(jnp.float32).reshape(seq_len, KVH, 2, HD)
    scores = jnp.einsum('tgjn,sgn->gjts', query_wide, pairs[:, :, 0], precision=highest) * HD ** (-0.5)
    causal = jnp.tril(jnp.ones((seq_len, seq_len), bool))
    spread = level[..., :, None] - level[..., None, :]
    decay = jnp.where(causal, jnp.exp(jnp.where(causal, spread, 0.0)), 0.0)
    mixed = jnp.einsum('gjts,sgn->tgjn', scores * decay * widths, pairs[:, :, 1], precision=highest)
    mixed = mixed + skip_gain.reshape(KVH, ratio)[None, :, :, None] * pairs[:, :, None, 1]
    return mixed.reshape(seq_len, QH * HD)

def reference(hidden_in, positions, assignment, query_weight, kv_weight, dt_weight, dt_bias, decay_log, skip_gain):
    group_rows = GROUP_SEQS * L
    rows_grouped = hidden_in.reshape(GROUPS, group_rows, D)
    spots_grouped = positions.reshape(GROUPS, group_rows)

    def one_group(items):
        rows, spots, order = items
        query, key_value, target = teacher_group(rows, spots, query_weight, kv_weight)

        def pick(values):
            shaped = values.reshape(GROUP_SEQS, L, values.shape[-1])
            return jnp.take(shaped, order.astype(jnp.int32), axis=0)
        return (pick(rows), pick(query), pick(key_value), pick(target))
    rows_s, query_s, pairs_s, target_s = lax.map(one_group, (rows_grouped, spots_grouped, assignment))
    rows_s = rows_s.reshape(SEQS, L, D)
    query_s = query_s.reshape(SEQS, L, QH * HD)
    pairs_s = pairs_s.reshape(SEQS, L, 2 * KVH * HD)
    target_s = target_s.reshape(SEQS, L, QH * HD)
    total = TOKENS * QH * HD

    def objective(weight_dt, bias_dt, log_decay, gain_skip):

        def one_seq(carry, items):
            rows, query, key_value, target = items
            mixed = student(weight_dt, bias_dt, log_decay, gain_skip, rows, query, key_value)
            differ = mixed - target.astype(jnp.float32)
            return (carry + jnp.sum(differ * differ) / total, mixed.astype(jnp.bfloat16))
        return lax.scan(jax.checkpoint(one_seq), jnp.zeros((), jnp.float32), (rows_s, query_s, pairs_s, target_s))
    loss, pullback, mixed = jax.vjp(objective, dt_weight, dt_bias, decay_log, skip_gain, has_aux=True)
    grads = pullback(jnp.ones((), jnp.float32))
    return (mixed.reshape(TOKENS, QH * HD), grads[0], grads[1], grads[2], grads[3], loss)
```

```python
import jax
import jax.numpy as jnp
from jax import lax
from jax.experimental import pallas as pl
from jax.experimental.pallas import tpu as pltpu
from jax.sharding import PartitionSpec as P

D = 8192
QH = 64
HD = 128
L = 128
RATIO = 8
CHUNKS = 8
CHIPS = 8
KB = 1024
TOTAL = 16384 * QH * HD
SCALE = HD**-0.5
KT = 384
NW = 1536
FAR = 4

highest = lax.Precision.HIGHEST
f32 = jnp.float32
bf16 = jnp.bfloat16


def dot_nt(a, b):
    return lax.dot_general(a, b, (((1,), (1,)), ((), ())), preferred_element_type=f32)


def dot_nn(a, b):
    return jnp.dot(a, b, preferred_element_type=f32)


def body(
    order,
    bias_s,
    decay_s,
    gain_s,
    positions,
    x_in,
    qw,
    kvw,
    dtw,
    out,
    gw_out,
    small_out,
    a_buf,
    w_buf,
    x_send,
    dt_stage,
    acc,
    qb,
    qt,
    s_t,
    s_s,
    n_buf,
    pb,
    o_buf,
    pre_t,
    gw,
    small,
    mixed,
    ex_ss,
    ex_rs,
    g_ss,
    g_rs,
    w_sem,
    wr_ss,
    wr_rs,
    o_ss,
    o_rs,
):
    me = lax.axis_index("mp")
    core = me % 2
    chip = me // 2
    x = chip // 4
    y = chip % 4
    xo = 1 - x
    up = (y + 1) % 4
    down = (y + 3) % 4
    across = (y + 2) % 4

    def device(xx, yy):
        return (xx * 4 + yy) * 2 + core

    partner = chip * 2 + (1 - core)
    to_up, to_down, to_x = device(x, up), device(x, down), device(xo, y)

    barrier = pltpu.get_barrier_semaphore()
    for step in range(1, 16):
        pl.semaphore_signal(barrier, inc=1, device_id={"mp": (me + step) % 16})
    pl.semaphore_wait(barrier, 15)

    q_cols = pl.ds(pl.multiple_of(core * 512, 512), 512)
    kv_cols = pl.ds(pl.multiple_of(1024 + core * 128, 128), 128)

    def remote(src, dst, ss, rs, dev):
        return pltpu.make_async_remote_copy(
            src_ref=src, dst_ref=dst, send_sem=ss, recv_sem=rs, device_id={"mp": dev}
        )

    def stage(i, carry):
        a_buf[i, chip, :, q_cols] = x_in[order[0, core * CHUNKS + i]]
        x_send[i] = x_in[order[0, (1 - core) * CHUNKS + i]]
        return carry

    lax.fori_loop(0, CHUNKS, stage, 0)

    def exchange(i):
        return remote(x_send.at[i], a_buf.at[i, chip, :, q_cols], ex_ss.at[i], ex_rs.at[i], partner)

    def start_exchange(i, carry):
        exchange(i).start()
        return carry

    lax.fori_loop(0, CHUNKS, start_exchange, 0)

    w_copies = (
        pltpu.make_async_copy(dtw, dt_stage, w_sem.at[2]),
        pltpu.make_async_copy(qw, w_buf.at[:, q_cols], w_sem.at[0]),
        pltpu.make_async_copy(kvw, w_buf.at[:, kv_cols], w_sem.at[1]),
    )
    w_remote = (
        remote(qw, w_buf.at[:, q_cols], wr_ss.at[0], wr_rs.at[0], partner),
        remote(kvw, w_buf.at[:, kv_cols], wr_ss.at[1], wr_rs.at[1], partner),
    )

    first = pl.ds(0, KT)
    second = pl.ds(KT, KB - KT)
    every = pl.ds(0, L)
    low = pl.ds(0, L // 2)
    high = pl.ds(L // 2, L // 2)
    whole = pl.ds(0, KB)

    def hop(kind, i):
        slot_x, slot_y, rows, cols, dev = (
            (x, y, every, whole, to_up),
            (x, y, every, whole, to_down),
            (x, y, every, whole, to_x),
            (x, down, low, first, to_up),
            (x, down, every, second, to_up),
            (x, down, every, first, to_x),
            (x, up, high, first, to_down),
            (x, up, every, first, to_x),
            (xo, y, every, second, to_up),
            (xo, y, every, second, to_down),
            (x, across, every, first, to_x),
            (xo, up, every, second, to_down),
        )[kind]
        ref = a_buf.at[i, slot_x * 4 + slot_y, rows, cols]
        return remote(ref, ref, g_ss.at[i, kind], g_rs.at[i, kind], dev)

    def hop1(i):
        exchange(i).wait_recv()
        for kind in (0, 1, 2):
            hop(kind, i).start()

    def hop2(i):
        hop(0, i).wait_recv()
        for kind in (4, 3, 5):
            hop(kind, i).start()
        hop(1, i).wait_recv()
        for kind in (6, 7):
            hop(kind, i).start()
        hop(2, i).wait_recv()
        for kind in (9, 8):
            hop(kind, i).start()

    def hop3(i):
        hop(9, i).wait_recv()
        hop(11, i).start()
        hop(3, i).wait_recv()
        hop(6, i).wait_recv()
        hop(10, i).start()

    def arrived(i):
        for kind in (4, 5, 7, 8, 10, 11):
            hop(kind, i).wait_recv()

    for i in range(FAR):
        hop1(i)
    for c in w_copies:
        c.start()
    for c in w_remote:
        c.start()

    w_copies[0].wait()

    def split_dt(r, carry):
        rows = pl.ds(pl.multiple_of(r * 512, 512), 512)
        w = dt_stage[rows, :]
        one = w.astype(bf16).astype(f32)
        left = w - one
        two = left.astype(bf16).astype(f32)
        three = left - two
        w_buf[rows, 1280:1408] = jnp.concatenate([one, two], axis=1).astype(bf16)
        w_buf[rows, 1408:1536] = jnp.concatenate([three, jnp.zeros_like(three)], axis=1).astype(bf16)
        return carry

    lax.fori_loop(0, D // 512, split_dt, 0)
    gw[...] = jnp.zeros_like(gw)
    small[...] = jnp.zeros_like(small)

    row_i = lax.broadcasted_iota(jnp.int32, (L, L), 0)
    col_i = lax.broadcasted_iota(jnp.int32, (L, L), 1)
    causal = col_i <= row_i
    upper = jnp.where(row_i <= col_i, 1.0, 0.0).astype(f32)
    lower = jnp.where(row_i >= col_i, 1.0, 0.0).astype(f32)
    head_row = lax.broadcasted_iota(jnp.int32, (RATIO, L), 0)

    def per_head(ref):
        values = jnp.zeros((RATIO, L), f32)
        for h in range(RATIO):
            values = jnp.where(head_row == h, ref[chip * RATIO + h], values)
        return values

    def out_copy(i):
        dst = out.at[:, pl.ds(pl.multiple_of(chip * KB, KB), KB)]
        target = core * CHUNKS + i

        def far():
            return remote(mixed.at[i], dst, o_ss.at[i], o_rs.at[chip], target)

        def near():
            return pltpu.make_async_copy(mixed.at[i], dst, o_rs.at[chip])

        return target, far, near

    def compute(i):
        def project(n, carry):
            cols = pl.ds(pl.multiple_of(n * 256, 256), 256)
            total = dot_nn(a_buf[i, 0], w_buf[0:KB, cols])
            for m in range(1, CHIPS):
                total += dot_nn(a_buf[i, m], w_buf[m * KB : (m + 1) * KB, cols])
            acc[:, cols] = total
            return carry

        lax.fori_loop(0, NW // 256, project, 0)

        spots = positions[pl.ds(order[0, core * CHUNKS + i], 1), :].astype(f32)
        spots = jnp.broadcast_to(spots, (L, L)).T
        lane = col_i % (HD // 2)
        frequency = jnp.exp(lane.astype(f32) * f32(-2.0 / HD * 13.122363377404328))
        angle = spots * frequency
        cosine = jnp.cos(angle)
        sine = jnp.where(col_i < HD // 2, -jnp.sin(angle), jnp.sin(angle))

        def rotate(head):
            wide = head.astype(f32)
            return (wide * cosine + pltpu.roll(wide, HD // 2, 1) * sine).astype(bf16)

        k = acc[:, 1024:1152].astype(bf16)
        v = acc[:, 1152:1280].astype(bf16)
        v32 = v.astype(f32)
        k_turned = rotate(k)
        for h in range(RATIO):
            rows = pl.ds(h * L, L)
            q = acc[:, h * HD : (h + 1) * HD].astype(bf16)
            qb[rows, :] = q
            qt[rows, :] = rotate(q)
        s_t[...] = dot_nt(qt[...], k_turned)
        s_s[...] = dot_nt(qb[...], k)
        for h in range(RATIO):
            rows = pl.ds(h * L, L)
            scores = jnp.where(causal, s_t[rows, :] * SCALE, -jnp.inf)
            weights = jnp.exp(scores - jnp.max(scores, axis=1, keepdims=True))
            pb[rows, :] = weights.astype(bf16)
        o_buf[...] = dot_nn(pb[...], jnp.concatenate([v, jnp.ones_like(v)], axis=1))

        pre = acc[:, 1280:1408] + acc[:, 1408:1536]
        pre = pre + pltpu.roll(pre, QH, 1)
        pre_t[...] = pre.T
        raw = pre_t[pl.ds(pl.multiple_of(chip * RATIO, RATIO), RATIO), :] + per_head(bias_s)
        step_size = jnp.maximum(raw, 0.0) + jnp.log1p(jnp.exp(-jnp.abs(raw)))
        rate = -jnp.exp(per_head(decay_s))
        summed = jnp.dot(step_size, upper, precision=highest, preferred_element_type=f32)
        level = rate * summed
        level_t = jnp.concatenate([level, jnp.zeros((L - RATIO, L), f32)], axis=0).T
        for h in range(RATIO):
            rows = pl.ds(h * L, L)
            spread = jnp.where(causal, level_t[:, h : h + 1] - level[h : h + 1, :], -jnp.inf)
            kept = s_s[rows, :] * SCALE * jnp.exp(spread)
            n_buf[rows, :] = kept
            pb[rows, :] = (kept * step_size[h : h + 1, :]).astype(bf16)
        s_s[...] = dot_nn(pb[...], v)
        gain_rows, loss_rows = [], []
        for h in range(RATIO):
            rows = pl.ds(h * L, L)
            teacher = o_buf[rows, :]
            target = (teacher[:, :HD] / teacher[:, HD:]).astype(bf16).astype(f32)
            value = s_s[rows, :] + gain_s[chip * RATIO + h] * v32
            mixed[i, :, h * HD : (h + 1) * HD] = value.astype(bf16)
            differ = value - target
            gain_rows.append(jnp.sum(differ * v32, axis=0, keepdims=True))
            loss_rows.append(jnp.sum(differ * differ, axis=0, keepdims=True))
            pb[rows, :] = differ.astype(bf16)
        target, far, near = out_copy(i)
        pl.when(target == me)(lambda: near().start())
        pl.when(target != me)(lambda: far().start())

        s_t[...] = dot_nt(pb[...], v)
        col_rows, row_cols = [], jnp.zeros((L, L), f32)
        for h in range(RATIO):
            rows = pl.ds(h * L, L)
            product = s_t[rows, :] * n_buf[rows, :]
            col_rows.append(jnp.sum(product, axis=0, keepdims=True))
            along = jnp.sum(product * step_size[h : h + 1, :], axis=1, keepdims=True)
            row_cols = jnp.where(col_i == h, along, row_cols)
        factor = f32(2.0 / TOTAL)
        by_col = jnp.concatenate(col_rows, axis=0) * factor
        by_row = row_cols.T[:RATIO, :] * factor
        d_level = by_row - step_size * by_col
        behind = jnp.dot(d_level, lower, precision=highest, preferred_element_type=f32)
        d_step = by_col + rate * behind
        d_raw = d_step * (1.0 / (1.0 + jnp.exp(-raw)))
        small[0:8, :] += d_raw
        small[8:16, :] += d_level * level
        small[16:24, :] += jnp.concatenate(gain_rows, axis=0) * factor
        small[24:32, :] += jnp.concatenate(loss_rows, axis=0) * f32(1.0 / TOTAL)
        upper_part = d_raw.astype(bf16).astype(f32)
        parts = jnp.concatenate([upper_part, d_raw - upper_part], axis=0).astype(bf16)
        for m in range(CHIPS):
            cols = slice(m * KB, (m + 1) * KB)
            gw[:, cols] += dot_nn(parts, a_buf[i, m])

    hop2(0)
    hop2(1)
    hop3(0)

    def phase(i, carry):
        pl.when(i + 1 < CHUNKS)(lambda: hop3(i + 1))
        pl.when(i + 2 < CHUNKS)(lambda: hop2(i + 2))
        pl.when(i + FAR < CHUNKS)(lambda: hop1(i + FAR))

        @pl.when(i == 0)
        def _():
            for c in w_copies[1:]:
                c.wait()
            for c in w_remote:
                c.wait_recv()

        arrived(i)
        compute(i)
        return carry

    lax.fori_loop(0, CHUNKS, phase, 0)

    gw_out[...] = gw[0:8, :] + gw[8:16, :]
    small_out[...] = small[...]

    def finish(i, carry):
        for kind in range(12):
            hop(kind, i).wait_send()
        exchange(i).wait_send()
        target, far, _ = out_copy(i)
        pl.when(target != me)(lambda: far().wait_send())
        dst = out.at[:, pl.ds(pl.multiple_of(i * KB, KB), KB)]
        pltpu.make_async_copy(mixed.at[i], dst, o_rs.at[i]).wait()
        return carry

    lax.fori_loop(0, CHUNKS, finish, 0)
    for c in w_remote:
        c.wait_send()


def fused(order, bias, decay, gain, positions, hidden, qw, kvw, dtw):
    smem = pl.BlockSpec(memory_space=pltpu.SMEM)
    vmem = pl.BlockSpec(memory_space=pltpu.VMEM)
    hbm = pl.BlockSpec(memory_space=pl.ANY)
    dma = pltpu.SemaphoreType.DMA
    stacked = (RATIO * L, HD)
    return pl.pallas_call(
        body,
        out_shape=(
            jax.ShapeDtypeStruct((L, D), bf16),
            jax.ShapeDtypeStruct((RATIO, D), f32),
            jax.ShapeDtypeStruct((32, L), f32),
        ),
        in_specs=[smem, smem, smem, smem, vmem, vmem, hbm, hbm, hbm],
        out_specs=(hbm, vmem, vmem),
        scratch_shapes=[
            pltpu.VMEM((CHUNKS, CHIPS, L, KB), bf16),
            pltpu.VMEM((D, NW), bf16),
            pltpu.VMEM((CHUNKS, L, 512), bf16),
            pltpu.VMEM((D, QH), f32),
            pltpu.VMEM((L, NW), f32),
            pltpu.VMEM(stacked, bf16),
            pltpu.VMEM(stacked, bf16),
            pltpu.VMEM(stacked, f32),
            pltpu.VMEM(stacked, f32),
            pltpu.VMEM(stacked, f32),
            pltpu.VMEM(stacked, bf16),
            pltpu.VMEM((RATIO * L, 2 * HD), f32),
            pltpu.VMEM((L, L), f32),
            pltpu.VMEM((16, D), f32),
            pltpu.VMEM((32, L), f32),
            pltpu.VMEM((CHUNKS, L, KB), bf16),
            dma((CHUNKS,)),
            dma((CHUNKS,)),
            dma((CHUNKS, 12)),
            dma((CHUNKS, 12)),
            dma((3,)),
            dma((2,)),
            dma((2,)),
            dma((CHUNKS,)),
            dma((CHIPS,)),
        ],
        name="fused",
        compiler_params=pltpu.CompilerParams(
            collective_id=0, has_side_effects=True, vmem_limit_bytes=60 * 2**20
        ),
    )(order, bias, decay, gain, positions, hidden, qw, kvw, dtw)


def local(
    hidden_in,
    positions,
    assignment,
    query_weight,
    kv_weight,
    dt_weight,
    dt_bias,
    decay_log,
    skip_gain,
):
    student_out, gw, small = fused(
        assignment,
        dt_bias,
        decay_log,
        skip_gain,
        positions.reshape(16, L),
        hidden_in.reshape(16, L, 512),
        query_weight,
        kv_weight,
        dt_weight,
    )
    sums = jnp.sum(small.reshape(4, RATIO, L), axis=2)
    gw, sums = lax.psum((gw, sums), "dp")
    gw = lax.all_gather(gw, "mp", axis=0)
    sums = lax.all_gather(sums, "mp", axis=0)
    gw = gw.reshape(CHIPS, 2, RATIO, D).sum(1).reshape(QH, D).T
    sums = sums.reshape(CHIPS, 2, 4, RATIO).sum(1).transpose(1, 0, 2).reshape(4, QH)
    return student_out, gw, sums[0], sums[1], sums[2], jnp.sum(sums[3])


def solution(mesh):
    placed = (
        P("dp", "mp"),
        P("dp"),
        P("dp", None),
        P(None, "mp"),
        P(None, "mp"),
        P(),
        P(),
        P(),
        P(),
    )
    return jax.shard_map(
        local,
        mesh=mesh,
        in_specs=placed,
        out_specs=(P(("dp", "mp"), None), P(), P(), P(), P(), P()),
        check_vma=False,
    )
```

```python
import jax
import jax.numpy as jnp
from jax import lax
from jax.experimental import pallas as pl
from jax.experimental.pallas import tpu as pltpu
from jax.sharding import PartitionSpec as P

D = 8192
QH = 64
HD = 128
L = 128
RATIO = 8
CHUNKS = 8
CHIPS = 8
KB = 1024
TOTAL = 16384 * QH * HD
SCALE = HD**-0.5
KT = 384
NW = 1280
PIECES = 16
PIECE = D // PIECES
PACK = PIECE + L
FAR = 4

highest = lax.Precision.HIGHEST
f32 = jnp.float32
bf16 = jnp.bfloat16


def dot_nt(a, b):
    return lax.dot_general(a, b, (((1,), (1,)), ((), ())), preferred_element_type=f32)


def dot_nn(a, b):
    return jnp.dot(a, b, preferred_element_type=f32)


def body(
    order,
    bias_s,
    decay_s,
    gain_s,
    positions,
    x_in,
    qw,
    kvw,
    dtw,
    out,
    gw_out,
    a_buf,
    w_buf,
    x_send,
    dt_stage,
    dt_parts,
    acc,
    qb,
    qt,
    s_t,
    s_s,
    n_buf,
    pb,
    o_buf,
    gw,
    small,
    mixed,
    ex_ss,
    ex_rs,
    g_ss,
    g_rs,
    w_sem,
    wr_ss,
    wr_rs,
    o_ss,
    o_rs,
):
    me = lax.axis_index("mp")
    core = me % 2
    chip = me // 2
    x = chip // 4
    y = chip % 4
    xo = 1 - x
    up = (y + 1) % 4
    down = (y + 3) % 4
    across = (y + 2) % 4

    def device(xx, yy):
        return (xx * 4 + yy) * 2 + core

    partner = chip * 2 + (1 - core)
    to_up, to_down, to_x = device(x, up), device(x, down), device(xo, y)

    barrier = pltpu.get_barrier_semaphore()
    for step in range(1, 16):
        pl.semaphore_signal(barrier, inc=1, device_id={"mp": (me + step) % 16})
    pl.semaphore_wait(barrier, 15)

    q_cols = pl.ds(pl.multiple_of(core * 512, 512), 512)
    kv_cols = pl.ds(pl.multiple_of(1024 + core * 128, 128), 128)

    def remote(src, dst, ss, rs, dev):
        return pltpu.make_async_remote_copy(
            src_ref=src, dst_ref=dst, send_sem=ss, recv_sem=rs, device_id={"mp": dev}
        )

    def stage(i, carry):
        a_buf[i, chip, :, q_cols] = x_in[order[0, core * CHUNKS + i]]
        x_send[i] = x_in[order[0, (1 - core) * CHUNKS + i]]
        return carry

    lax.fori_loop(0, CHUNKS, stage, 0)

    def exchange(i):
        return remote(x_send.at[i], a_buf.at[i, chip, :, q_cols], ex_ss.at[i], ex_rs.at[i], partner)

    def start_exchange(i, carry):
        exchange(i).start()
        return carry

    lax.fori_loop(0, CHUNKS, start_exchange, 0)

    w_copies = (
        pltpu.make_async_copy(
            dtw.at[pl.ds(pl.multiple_of(chip * RATIO, RATIO), RATIO), :], dt_stage, w_sem.at[2]
        ),
        pltpu.make_async_copy(qw, w_buf.at[:, q_cols], w_sem.at[0]),
        pltpu.make_async_copy(kvw, w_buf.at[:, kv_cols], w_sem.at[1]),
    )
    w_remote = (
        remote(qw, w_buf.at[:, q_cols], wr_ss.at[0], wr_rs.at[0], partner),
        remote(kvw, w_buf.at[:, kv_cols], wr_ss.at[1], wr_rs.at[1], partner),
    )

    first = pl.ds(0, KT)
    second = pl.ds(KT, KB - KT)
    every = pl.ds(0, L)
    low = pl.ds(0, L // 2)
    high = pl.ds(L // 2, L // 2)
    whole = pl.ds(0, KB)

    def hop(kind, i):
        slot_x, slot_y, rows, cols, dev = (
            (x, y, every, whole, to_up),
            (x, y, every, whole, to_down),
            (x, y, every, whole, to_x),
            (x, down, low, first, to_up),
            (x, down, every, second, to_up),
            (x, down, every, first, to_x),
            (x, up, high, first, to_down),
            (x, up, every, first, to_x),
            (xo, y, every, second, to_up),
            (xo, y, every, second, to_down),
            (x, across, every, first, to_x),
            (xo, up, every, second, to_down),
        )[kind]
        ref = a_buf.at[i, slot_x * 4 + slot_y, rows, cols]
        return remote(ref, ref, g_ss.at[i, kind], g_rs.at[i, kind], dev)

    def hop1(i):
        exchange(i).wait_recv()
        for kind in (0, 1, 2):
            hop(kind, i).start()

    def hop2(i):
        hop(0, i).wait_recv()
        for kind in (4, 3, 5):
            hop(kind, i).start()
        hop(1, i).wait_recv()
        for kind in (6, 7):
            hop(kind, i).start()
        hop(2, i).wait_recv()
        for kind in (9, 8):
            hop(kind, i).start()

    def hop3(i):
        hop(9, i).wait_recv()
        hop(11, i).start()
        hop(3, i).wait_recv()
        hop(6, i).wait_recv()
        hop(10, i).start()

    def arrived(i):
        for kind in (4, 5, 7, 8, 10, 11):
            hop(kind, i).wait_recv()

    for i in range(FAR):
        hop1(i)
    for c in w_copies:
        c.start()
    for c in w_remote:
        c.start()

    w_copies[0].wait()
    w = dt_stage[...]
    one = w.astype(bf16).astype(f32)
    two = (w - one).astype(bf16).astype(f32)
    three = w - one - two
    dt_parts[...] = jnp.concatenate([one, two, three, jnp.zeros_like(w)], axis=0).astype(bf16)
    gw[...] = jnp.zeros_like(gw)
    small[...] = jnp.zeros_like(small)

    row_i = lax.broadcasted_iota(jnp.int32, (L, L), 0)
    col_i = lax.broadcasted_iota(jnp.int32, (L, L), 1)
    causal = col_i <= row_i
    upper = jnp.where(row_i <= col_i, 1.0, 0.0).astype(f32)
    lower = jnp.where(row_i >= col_i, 1.0, 0.0).astype(f32)
    head_row = lax.broadcasted_iota(jnp.int32, (RATIO, L), 0)

    def per_head(ref):
        values = jnp.zeros((RATIO, L), f32)
        for h in range(RATIO):
            values = jnp.where(head_row == h, ref[chip * RATIO + h], values)
        return values

    def out_copy(i):
        dst = out.at[:, pl.ds(pl.multiple_of(chip * KB, KB), KB)]
        target = core * CHUNKS + i

        def far():
            return remote(mixed.at[i], dst, o_ss.at[i], o_rs.at[chip], target)

        def near():
            return pltpu.make_async_copy(mixed.at[i], dst, o_rs.at[chip])

        return target, far, near

    def compute(i):
        def project(n, carry):
            cols = pl.ds(pl.multiple_of(n * 256, 256), 256)
            total = dot_nn(a_buf[i, 0], w_buf[0:KB, cols])
            for m in range(1, CHIPS):
                total += dot_nn(a_buf[i, m], w_buf[m * KB : (m + 1) * KB, cols])
            acc[:, cols] = total
            return carry

        lax.fori_loop(0, NW // 256, project, 0)

        spots = positions[pl.ds(order[0, core * CHUNKS + i], 1), :].astype(f32)
        spots = jnp.broadcast_to(spots, (L, L)).T
        lane = col_i % (HD // 2)
        frequency = jnp.exp(lane.astype(f32) * f32(-2.0 / HD * 13.122363377404328))
        angle = spots * frequency
        cosine = jnp.cos(angle)
        sine = jnp.where(col_i < HD // 2, -jnp.sin(angle), jnp.sin(angle))

        def rotate(head):
            wide = head.astype(f32)
            return (wide * cosine + pltpu.roll(wide, HD // 2, 1) * sine).astype(bf16)

        k = acc[:, 1024:1152].astype(bf16)
        v = acc[:, 1152:1280].astype(bf16)
        v32 = v.astype(f32)
        k_turned = rotate(k)
        for h in range(RATIO):
            rows = pl.ds(h * L, L)
            q = acc[:, h * HD : (h + 1) * HD].astype(bf16)
            qb[rows, :] = q
            qt[rows, :] = rotate(q)
        s_t[...] = dot_nt(qt[...], k_turned)
        s_s[...] = dot_nt(qb[...], k)
        for h in range(RATIO):
            rows = pl.ds(h * L, L)
            scores = jnp.where(causal, s_t[rows, :] * SCALE, -jnp.inf)
            weights = jnp.exp(scores - jnp.max(scores, axis=1, keepdims=True))
            pb[rows, :] = weights.astype(bf16)
        o_buf[...] = dot_nn(pb[...], jnp.concatenate([v, jnp.ones_like(v)], axis=1))

        pre = dot_nt(dt_parts[:, 0:KB], a_buf[i, 0])
        for m in range(1, CHIPS):
            pre += dot_nt(dt_parts[:, m * KB : (m + 1) * KB], a_buf[i, m])
        raw = pre[0:8] + pre[8:16] + pre[16:24] + per_head(bias_s)
        step_size = jnp.maximum(raw, 0.0) + jnp.log1p(jnp.exp(-jnp.abs(raw)))
        rate = -jnp.exp(per_head(decay_s))
        summed = jnp.dot(step_size, upper, precision=highest, preferred_element_type=f32)
        level = rate * summed
        level_t = jnp.concatenate([level, jnp.zeros((L - RATIO, L), f32)], axis=0).T
        for h in range(RATIO):
            rows = pl.ds(h * L, L)
            spread = jnp.where(causal, level_t[:, h : h + 1] - level[h : h + 1, :], -jnp.inf)
            kept = s_s[rows, :] * SCALE * jnp.exp(spread)
            n_buf[rows, :] = kept
            pb[rows, :] = (kept * step_size[h : h + 1, :]).astype(bf16)
        s_s[...] = dot_nn(pb[...], v)
        gain_rows, loss_rows = [], []
        for h in range(RATIO):
            rows = pl.ds(h * L, L)
            teacher = o_buf[rows, :]
            target = (teacher[:, :HD] / teacher[:, HD:]).astype(bf16).astype(f32)
            value = s_s[rows, :] + gain_s[chip * RATIO + h] * v32
            mixed[i, :, h * HD : (h + 1) * HD] = value.astype(bf16)
            differ = value - target
            gain_rows.append(jnp.sum(differ * v32, axis=0, keepdims=True))
            loss_rows.append(jnp.sum(differ * differ, axis=0, keepdims=True))
            pb[rows, :] = differ.astype(bf16)
        target, far, near = out_copy(i)
        pl.when(target == me)(lambda: near().start())
        pl.when(target != me)(lambda: far().start())

        s_t[...] = dot_nt(pb[...], v)
        col_rows, row_cols = [], jnp.zeros((L, L), f32)
        for h in range(RATIO):
            rows = pl.ds(h * L, L)
            product = s_t[rows, :] * n_buf[rows, :]
            col_rows.append(jnp.sum(product, axis=0, keepdims=True))
            along = jnp.sum(product * step_size[h : h + 1, :], axis=1, keepdims=True)
            row_cols = jnp.where(col_i == h, along, row_cols)
        factor = f32(2.0 / TOTAL)
        by_col = jnp.concatenate(col_rows, axis=0) * factor
        by_row = row_cols.T[:RATIO, :] * factor
        d_level = by_row - step_size * by_col
        behind = jnp.dot(d_level, lower, precision=highest, preferred_element_type=f32)
        d_step = by_col + rate * behind
        d_raw = d_step * (1.0 / (1.0 + jnp.exp(-raw)))
        small[0:8, :] += d_raw
        small[8:16, :] += d_level * level
        small[16:24, :] += jnp.concatenate(gain_rows, axis=0) * factor
        small[24:32, :] += jnp.concatenate(loss_rows, axis=0) * f32(1.0 / TOTAL)
        upper_part = d_raw.astype(bf16).astype(f32)
        parts = jnp.concatenate([upper_part, d_raw - upper_part], axis=0).astype(bf16)
        for m in range(CHIPS):
            cols = slice(m * KB, (m + 1) * KB)
            gw[:, cols] += dot_nn(parts, a_buf[i, m])

    hop2(0)
    hop2(1)
    hop3(0)

    def phase(i, carry):
        pl.when(i + 1 < CHUNKS)(lambda: hop3(i + 1))
        pl.when(i + 2 < CHUNKS)(lambda: hop2(i + 2))
        pl.when(i + FAR < CHUNKS)(lambda: hop1(i + FAR))

        @pl.when(i == 0)
        def _():
            for c in w_copies[1:]:
                c.wait()
            for c in w_remote:
                c.wait_recv()

        arrived(i)
        compute(i)
        return carry

    lax.fori_loop(0, CHUNKS, phase, 0)

    packed = jnp.zeros((RATIO, L), f32)
    for n in range(4):
        line = jnp.sum(small[n * RATIO : (n + 1) * RATIO, :], axis=1, keepdims=True)
        packed = jnp.where(col_i[:RATIO] == n, line, packed)
    for r in range(PIECES):
        cols = slice(r * PIECE, (r + 1) * PIECE)
        gw_out[r, :, 0:PIECE] = gw[0:8, cols] + gw[8:16, cols]
        gw_out[r, :, PIECE:PACK] = packed

    def finish(i, carry):
        for kind in range(12):
            hop(kind, i).wait_send()
        exchange(i).wait_send()
        target, far, _ = out_copy(i)
        pl.when(target != me)(lambda: far().wait_send())
        dst = out.at[:, pl.ds(pl.multiple_of(i * KB, KB), KB)]
        pltpu.make_async_copy(mixed.at[i], dst, o_rs.at[i]).wait()
        return carry

    lax.fori_loop(0, CHUNKS, finish, 0)
    for c in w_remote:
        c.wait_send()


def fused(order, bias, decay, gain, positions, hidden, qw, kvw, dtw):
    smem = pl.BlockSpec(memory_space=pltpu.SMEM)
    vmem = pl.BlockSpec(memory_space=pltpu.VMEM)
    hbm = pl.BlockSpec(memory_space=pl.ANY)
    dma = pltpu.SemaphoreType.DMA
    stacked = (RATIO * L, HD)
    return pl.pallas_call(
        body,
        out_shape=(
            jax.ShapeDtypeStruct((L, D), bf16),
            jax.ShapeDtypeStruct((PIECES, RATIO, PACK), f32),
        ),
        in_specs=[smem, smem, smem, smem, vmem, vmem, hbm, hbm, hbm],
        out_specs=(hbm, vmem),
        scratch_shapes=[
            pltpu.VMEM((CHUNKS, CHIPS, L, KB), bf16),
            pltpu.VMEM((D, NW), bf16),
            pltpu.VMEM((CHUNKS, L, 512), bf16),
            pltpu.VMEM((RATIO, D), f32),
            pltpu.VMEM((32, D), bf16),
            pltpu.VMEM((L, NW), f32),
            pltpu.VMEM(stacked, bf16),
            pltpu.VMEM(stacked, bf16),
            pltpu.VMEM(stacked, f32),
            pltpu.VMEM(stacked, f32),
            pltpu.VMEM(stacked, f32),
            pltpu.VMEM(stacked, bf16),
            pltpu.VMEM((RATIO * L, 2 * HD), f32),
            pltpu.VMEM((16, D), f32),
            pltpu.VMEM((32, L), f32),
            pltpu.VMEM((CHUNKS, L, KB), bf16),
            dma((CHUNKS,)),
            dma((CHUNKS,)),
            dma((CHUNKS, 12)),
            dma((CHUNKS, 12)),
            dma((3,)),
            dma((2,)),
            dma((2,)),
            dma((CHUNKS,)),
            dma((CHIPS,)),
        ],
        name="fused",
        compiler_params=pltpu.CompilerParams(
            collective_id=0, has_side_effects=True, vmem_limit_bytes=60 * 2**20
        ),
    )(order, bias, decay, gain, positions, hidden, qw, kvw, dtw)


def reduce_body(
    mine,
    grad,
    rows,
    loss,
    got,
    own,
    heads,
    narrow,
    s1s,
    s1r,
    s2s,
    s2r,
    s3s,
    s3r,
    s4s,
    s4r,
):
    d = lax.axis_index("dp")
    me = lax.axis_index("mp")
    core = me % 2
    chip = me // 2
    place = d * 2 + core

    def same_chip(step):
        r = (place + step) % PIECES
        return {"dp": r // 2, "mp": chip * 2 + r % 2}

    def same_core(step):
        return {"dp": d, "mp": (chip + step) % CHIPS * 2 + core}

    barrier = pltpu.get_barrier_semaphore()
    for step in range(1, PIECES):
        pl.semaphore_signal(barrier, inc=1, device_id=same_chip(step))
    for step in range(1, CHIPS):
        pl.semaphore_signal(barrier, inc=1, device_id=same_core(step))
    pl.semaphore_wait(barrier, PIECES + CHIPS - 2)

    def scatter(step):
        return pltpu.make_async_remote_copy(
            src_ref=mine.at[(place + step) % PIECES],
            dst_ref=got.at[step],
            send_sem=s1s.at[step],
            recv_sem=s1r.at[step],
            device_id=same_chip(step),
        )

    for step in range(1, PIECES):
        scatter(step).start()
    total = mine[place]
    for step in range(1, PIECES):
        scatter(step).wait_recv()
        total += got[step]
    own[...] = total

    def across_heads(step):
        return pltpu.make_async_remote_copy(
            src_ref=own,
            dst_ref=heads.at[chip],
            send_sem=s2s.at[step],
            recv_sem=s2r.at[step],
            device_id=same_core(step),
        )

    for step in range(1, CHIPS):
        across_heads(step).start()
    heads[chip] = total
    for step in range(1, CHIPS):
        across_heads(step).wait_recv()
    narrow[core, d] = heads[:, :, 0:PIECE].reshape(QH, PIECE).astype(bf16)

    def pieces(step):
        return pltpu.make_async_remote_copy(
            src_ref=narrow.at[core, d],
            dst_ref=narrow.at[core, d],
            send_sem=s3s.at[step],
            recv_sem=s3r.at[step],
            device_id={"dp": (d + step) % 8, "mp": me},
        )

    def to_partner(step):
        ref = narrow.at[core, (d + 8 - step) % 8]
        return pltpu.make_async_remote_copy(
            src_ref=ref,
            dst_ref=ref,
            send_sem=s4s.at[step],
            recv_sem=s4r.at[step],
            device_id={"dp": d, "mp": chip * 2 + 1 - core},
        )

    for step in range(1, 8):
        pieces(step).start()
    to_partner(0).start()
    lines = heads[:, :, PIECE:PACK].reshape(QH, L)
    lines = jnp.concatenate([lines, jnp.zeros_like(lines)], axis=0).T
    rows[...] = lines[0:8, :]
    loss[0, 0] = jnp.sum(lines[3:4, :])
    for step in range(1, 8):
        pieces(step).wait_recv()
        to_partner(step).start()
    for step in range(8):
        to_partner(step).wait_recv()
    for r in range(PIECES):
        grad[:, r * PIECE : (r + 1) * PIECE] = narrow[r % 2, r // 2].astype(f32)
    for step in range(1, PIECES):
        scatter(step).wait_send()
    for step in range(1, CHIPS):
        across_heads(step).wait_send()
    for step in range(1, 8):
        pieces(step).wait_send()
    for step in range(8):
        to_partner(step).wait_send()


def reduce_all(mine):
    vmem = pl.BlockSpec(memory_space=pltpu.VMEM)
    dma = pltpu.SemaphoreType.DMA
    return pl.pallas_call(
        reduce_body,
        out_shape=(
            jax.ShapeDtypeStruct((QH, D), f32),
            jax.ShapeDtypeStruct((8, L), f32),
            jax.ShapeDtypeStruct((1, 1), f32),
        ),
        in_specs=[vmem],
        out_specs=(vmem, vmem, pl.BlockSpec(memory_space=pltpu.SMEM)),
        scratch_shapes=[
            pltpu.VMEM((PIECES, RATIO, PACK), f32),
            pltpu.VMEM((RATIO, PACK), f32),
            pltpu.VMEM((CHIPS, RATIO, PACK), f32),
            pltpu.VMEM((2, 8, QH, PIECE), bf16),
            dma((PIECES,)),
            dma((PIECES,)),
            dma((CHIPS,)),
            dma((CHIPS,)),
            dma((8,)),
            dma((8,)),
            dma((8,)),
            dma((8,)),
        ],
        name="reduce_all",
        compiler_params=pltpu.CompilerParams(
            collective_id=1, has_side_effects=True, vmem_limit_bytes=32 * 2**20
        ),
    )(mine)


def local(
    hidden_in,
    positions,
    assignment,
    query_weight,
    kv_weight,
    dt_weight,
    dt_bias,
    decay_log,
    skip_gain,
):
    student_out, partial = fused(
        assignment,
        dt_bias,
        decay_log,
        skip_gain,
        positions.reshape(16, L),
        hidden_in.reshape(16, L, 512),
        query_weight,
        kv_weight,
        dt_weight.T,
    )
    grad, rows, loss = reduce_all(partial)
    return student_out, grad.T, rows[0, :QH], rows[1, :QH], rows[2, :QH], loss.reshape(())


def solution(mesh):
    placed = (
        P("dp", "mp"),
        P("dp"),
        P("dp", None),
        P(None, "mp"),
        P(None, "mp"),
        P(),
        P(),
        P(),
        P(),
    )
    return jax.shard_map(
        local,
        mesh=mesh,
        in_specs=placed,
        out_specs=(P(("dp", "mp"), None), P(), P(), P(), P(), P()),
        check_vma=False,
    )
```

```python
import jax
import jax.numpy as jnp
from jax import lax
from jax.experimental import pallas as pl
from jax.experimental.pallas import tpu as pltpu
from jax.sharding import PartitionSpec as P

D = 8192
QH = 64
HD = 128
L = 128
RATIO = 8
CHUNKS = 8
CHIPS = 8
KB = 1024
TOTAL = 16384 * QH * HD
SCALE = HD**-0.5
KT = 512
NW = 1280
PIECES = 16
PIECE = D // PIECES
PACK = PIECE + L
FAR = 4
SHIFT = 4

highest = lax.Precision.HIGHEST
f32 = jnp.float32
bf16 = jnp.bfloat16


def dot_nt(a, b):
    return lax.dot_general(a, b, (((1,), (1,)), ((), ())), preferred_element_type=f32)


def dot_nn(a, b):
    return jnp.dot(a, b, preferred_element_type=f32)


def body(
    order,
    bias_s,
    decay_s,
    gain_s,
    positions,
    x_in,
    qw,
    kvw,
    dtw,
    out,
    narrow,
    rows_out,
    loss_out,
    mine,
    a_buf,
    w_buf,
    x_send,
    dt_stage,
    dt_parts,
    acc,
    qb,
    qt,
    s_t,
    s_s,
    n_buf,
    pb,
    o_buf,
    gw,
    small,
    mixed,
    ex_ss,
    ex_rs,
    g_ss,
    g_rs,
    w_sem,
    wr_ss,
    wr_rs,
    o_ss,
    o_rs,
    got,
    own,
    heads,
    s1s,
    s1r,
    s2s,
    s2r,
    s3s,
    s3r,
    s4s,
    s4r,
):
    me = lax.axis_index("mp")
    core = me % 2
    chip = me // 2
    x = chip // 4
    y = chip % 4
    xo = 1 - x
    up = (y + 1) % 4
    down = (y + 3) % 4
    across = (y + 2) % 4

    def device(xx, yy):
        return (xx * 4 + yy) * 2 + core

    def block(which, i):
        return which * CHUNKS + (i + SHIFT * which) % CHUNKS

    lag = (y + 2 * x) % 4

    partner = chip * 2 + (1 - core)
    to_up, to_down, to_x = device(x, up), device(x, down), device(xo, y)

    d = lax.axis_index("dp")
    place = d * 2 + core

    def same_chip(step):
        r = (place + step) % PIECES
        return {"dp": r // 2, "mp": chip * 2 + r % 2}

    def same_core(step):
        return {"dp": d, "mp": (chip + step) % CHIPS * 2 + core}

    barrier = pltpu.get_barrier_semaphore()
    for step in range(1, 16):
        pl.semaphore_signal(barrier, inc=1, device_id={"dp": d, "mp": (me + step) % 16})
    for step in range(1, PIECES):
        pl.semaphore_signal(barrier, inc=1, device_id=same_chip(step))
    pl.semaphore_wait(barrier, 30)

    q_cols = pl.ds(pl.multiple_of(core * 512, 512), 512)
    kv_cols = pl.ds(pl.multiple_of(1024 + core * 128, 128), 128)

    def remote(src, dst, ss, rs, dev):
        return pltpu.make_async_remote_copy(
            src_ref=src, dst_ref=dst, send_sem=ss, recv_sem=rs, device_id={"mp": dev}
        )

    def stage(i, carry):
        a_buf[i, chip, :, q_cols] = x_in[order[0, block(core, i)]]
        x_send[i] = x_in[order[0, block(1 - core, i)]]
        return carry

    lax.fori_loop(0, CHUNKS, stage, 0)

    def exchange(i):
        return remote(x_send.at[i], a_buf.at[i, chip, :, q_cols], ex_ss.at[i], ex_rs.at[i], partner)

    def start_exchange(i, carry):
        exchange(i).start()
        return carry

    lax.fori_loop(0, CHUNKS, start_exchange, 0)

    w_copies = (
        pltpu.make_async_copy(
            dtw.at[pl.ds(pl.multiple_of(chip * RATIO, RATIO), RATIO), :], dt_stage, w_sem.at[2]
        ),
        pltpu.make_async_copy(qw, w_buf.at[:, q_cols], w_sem.at[0]),
        pltpu.make_async_copy(kvw, w_buf.at[:, kv_cols], w_sem.at[1]),
    )
    w_remote = (
        remote(qw, w_buf.at[:, q_cols], wr_ss.at[0], wr_rs.at[0], partner),
        remote(kvw, w_buf.at[:, kv_cols], wr_ss.at[1], wr_rs.at[1], partner),
    )

    first = pl.ds(0, KT)
    second = pl.ds(KT, KB - KT)
    every = pl.ds(0, L)
    whole = pl.ds(0, KB)

    def hop(kind, i):
        slot_x, slot_y, rows, cols, dev = (
            (x, y, every, whole, to_up),
            (x, y, every, whole, to_down),
            (x, y, every, whole, to_x),
            (x, down, every, second, to_up),
            (x, down, every, first, to_x),
            (x, up, every, first, to_down),
            (x, up, every, first, to_x),
            (xo, y, every, second, to_up),
            (xo, y, every, second, to_down),
            (x, across, every, first, to_x),
            (xo, up, every, second, to_down),
        )[kind]
        ref = a_buf.at[i, slot_x * 4 + slot_y, rows, cols]
        return remote(ref, ref, g_ss.at[i, kind], g_rs.at[i, kind], dev)

    def hop1(i):
        exchange(i).wait_recv()
        for kind in (0, 1, 2):
            hop(kind, i).start()

    def hop2(i):
        hop(0, i).wait_recv()
        for kind in (3, 4):
            hop(kind, i).start()
        hop(1, i).wait_recv()
        for kind in (5, 6):
            hop(kind, i).start()
        hop(2, i).wait_recv()
        for kind in (8, 7):
            hop(kind, i).start()

    def hop3(i):
        hop(8, i).wait_recv()
        hop(10, i).start()
        hop(5, i).wait_recv()
        hop(9, i).start()

    def arrived(i):
        for kind in (3, 4, 6, 7, 9, 10):
            hop(kind, i).wait_recv()

    for i in range(FAR):
        hop1(i)
    for c in w_copies:
        c.start()
    for c in w_remote:
        c.start()

    w_copies[0].wait()
    w = dt_stage[...]
    one = w.astype(bf16).astype(f32)
    two = (w - one).astype(bf16).astype(f32)
    three = w - one - two
    dt_parts[...] = jnp.concatenate([one, two, three, jnp.zeros_like(w)], axis=0).astype(bf16)
    gw[...] = jnp.zeros_like(gw)
    small[...] = jnp.zeros_like(small)

    row_i = lax.broadcasted_iota(jnp.int32, (L, L), 0)
    col_i = lax.broadcasted_iota(jnp.int32, (L, L), 1)
    causal = col_i <= row_i
    upper = jnp.where(row_i <= col_i, 1.0, 0.0).astype(f32)
    lower = jnp.where(row_i >= col_i, 1.0, 0.0).astype(f32)
    head_row = lax.broadcasted_iota(jnp.int32, (RATIO, L), 0)

    def per_head(ref):
        values = jnp.zeros((RATIO, L), f32)
        for h in range(RATIO):
            values = jnp.where(head_row == h, ref[chip * RATIO + h], values)
        return values

    def out_copy(i):
        dst = out.at[:, pl.ds(pl.multiple_of(chip * KB, KB), KB)]
        target = block(core, i)

        def far():
            return remote(mixed.at[i], dst, o_ss.at[i], o_rs.at[chip], target)

        def near():
            return pltpu.make_async_copy(mixed.at[i], dst, o_rs.at[chip])

        return target, far, near

    def send_out(i):
        target, far, near = out_copy(i)
        pl.when(target == me)(lambda: near().start())
        pl.when(target != me)(lambda: far().start())

    def compute(i):
        def project(n, carry):
            cols = pl.ds(pl.multiple_of(n * 256, 256), 256)
            total = dot_nn(a_buf[i, 0], w_buf[0:KB, cols])
            for m in range(1, CHIPS):
                total += dot_nn(a_buf[i, m], w_buf[m * KB : (m + 1) * KB, cols])
            acc[:, cols] = total
            return carry

        lax.fori_loop(0, NW // 256, project, 0)

        spots = positions[pl.ds(order[0, block(core, i)], 1), :].astype(f32)
        spots = jnp.broadcast_to(spots, (L, L)).T
        lane = col_i % (HD // 2)
        frequency = jnp.exp(lane.astype(f32) * f32(-2.0 / HD * 13.122363377404328))
        angle = spots * frequency
        cosine = jnp.cos(angle)
        sine = jnp.where(col_i < HD // 2, -jnp.sin(angle), jnp.sin(angle))

        def rotate(head):
            wide = head.astype(f32)
            return (wide * cosine + pltpu.roll(wide, HD // 2, 1) * sine).astype(bf16)

        k = acc[:, 1024:1152].astype(bf16)
        v = acc[:, 1152:1280].astype(bf16)
        v32 = v.astype(f32)
        k_turned = rotate(k)
        for h in range(RATIO):
            rows = pl.ds(h * L, L)
            q = acc[:, h * HD : (h + 1) * HD].astype(bf16)
            qb[rows, :] = q
            qt[rows, :] = rotate(q)
        s_t[...] = dot_nt(qt[...], k_turned)
        s_s[...] = dot_nt(qb[...], k)
        for h in range(RATIO):
            rows = pl.ds(h * L, L)
            scores = jnp.where(causal, s_t[rows, :] * SCALE, -jnp.inf)
            weights = jnp.exp(scores - jnp.max(scores, axis=1, keepdims=True))
            pb[rows, :] = weights.astype(bf16)
        o_buf[...] = dot_nn(pb[...], jnp.concatenate([v, jnp.ones_like(v)], axis=1))

        pre = dot_nt(dt_parts[:, 0:KB], a_buf[i, 0])
        for m in range(1, CHIPS):
            pre += dot_nt(dt_parts[:, m * KB : (m + 1) * KB], a_buf[i, m])
        raw = pre[0:8] + pre[8:16] + pre[16:24] + per_head(bias_s)
        step_size = jnp.maximum(raw, 0.0) + jnp.log1p(jnp.exp(-jnp.abs(raw)))
        rate = -jnp.exp(per_head(decay_s))
        summed = jnp.dot(step_size, upper, precision=highest, preferred_element_type=f32)
        level = rate * summed
        level_t = jnp.concatenate([level, jnp.zeros((L - RATIO, L), f32)], axis=0).T
        for h in range(RATIO):
            rows = pl.ds(h * L, L)
            spread = jnp.where(causal, level_t[:, h : h + 1] - level[h : h + 1, :], -jnp.inf)
            kept = s_s[rows, :] * SCALE * jnp.exp(spread)
            n_buf[rows, :] = kept
            pb[rows, :] = (kept * step_size[h : h + 1, :]).astype(bf16)
        s_s[...] = dot_nn(pb[...], v)
        gain_rows, loss_rows = [], []
        for h in range(RATIO):
            rows = pl.ds(h * L, L)
            teacher = o_buf[rows, :]
            target = (teacher[:, :HD] / teacher[:, HD:]).astype(bf16).astype(f32)
            value = s_s[rows, :] + gain_s[chip * RATIO + h] * v32
            mixed[i, :, h * HD : (h + 1) * HD] = value.astype(bf16)
            differ = value - target
            gain_rows.append(jnp.sum(differ * v32, axis=0, keepdims=True))
            loss_rows.append(jnp.sum(differ * differ, axis=0, keepdims=True))
            pb[rows, :] = differ.astype(bf16)

        @pl.when(i >= lag)
        def _():
            send_out(i - lag)

        s_t[...] = dot_nt(pb[...], v)
        col_rows, row_cols = [], jnp.zeros((L, L), f32)
        for h in range(RATIO):
            rows = pl.ds(h * L, L)
            product = s_t[rows, :] * n_buf[rows, :]
            col_rows.append(jnp.sum(product, axis=0, keepdims=True))
            along = jnp.sum(product * step_size[h : h + 1, :], axis=1, keepdims=True)
            row_cols = jnp.where(col_i == h, along, row_cols)
        factor = f32(2.0 / TOTAL)
        by_col = jnp.concatenate(col_rows, axis=0) * factor
        by_row = row_cols.T[:RATIO, :] * factor
        d_level = by_row - step_size * by_col
        behind = jnp.dot(d_level, lower, precision=highest, preferred_element_type=f32)
        d_step = by_col + rate * behind
        d_raw = d_step * (1.0 / (1.0 + jnp.exp(-raw)))
        small[0:8, :] += d_raw
        small[8:16, :] += d_level * level
        small[16:24, :] += jnp.concatenate(gain_rows, axis=0) * factor
        small[24:32, :] += jnp.concatenate(loss_rows, axis=0) * f32(1.0 / TOTAL)
        upper_part = d_raw.astype(bf16).astype(f32)
        parts = jnp.concatenate([upper_part, d_raw - upper_part], axis=0).astype(bf16)
        for m in range(CHIPS):
            cols = slice(m * KB, (m + 1) * KB)
            gw[:, cols] += dot_nn(parts, a_buf[i, m])

    def scatter(step):
        return pltpu.make_async_remote_copy(
            src_ref=mine.at[(place + step) % PIECES],
            dst_ref=got.at[step],
            send_sem=s1s.at[step],
            recv_sem=s1r.at[step],
            device_id=same_chip(step),
        )

    def across_heads(step):
        return pltpu.make_async_remote_copy(
            src_ref=own,
            dst_ref=heads.at[chip],
            send_sem=s2s.at[step],
            recv_sem=s2r.at[step],
            device_id=same_core(step),
        )

    def columns(dd):
        at = (dd * 2 + core) * PIECE
        return narrow.at[:, pl.ds(pl.multiple_of(at, PIECE), PIECE)]

    def pieces(step):
        return pltpu.make_async_remote_copy(
            src_ref=columns(d),
            dst_ref=columns(d),
            send_sem=s3s.at[step],
            recv_sem=s3r.at[step],
            device_id={"dp": (d + step) % 8, "mp": me},
        )

    def to_partner(step):
        ref = columns((d + 8 - step) % 8)
        return remote(ref, ref, s4s.at[step], s4r.at[step], partner)

    def sum_up():
        for step in range(1, PIECES):
            scatter(step).start()
        total = mine[place]
        for step in range(1, PIECES):
            scatter(step).wait_recv()
            total += got[step]
        own[...] = total
        for step in range(1, CHIPS):
            across_heads(step).start()
        heads[chip] = total
        for step in range(1, CHIPS):
            across_heads(step).wait_recv()
        at = pl.multiple_of(place * PIECE, PIECE)
        narrow[:, pl.ds(at, PIECE)] = heads[:, :, 0:PIECE].reshape(QH, PIECE).astype(bf16)
        for step in range(1, 8):
            pieces(step).start()
        to_partner(0).start()
        lines = heads[:, :, PIECE:PACK].reshape(QH, L)
        lines = jnp.concatenate([lines, jnp.zeros_like(lines)], axis=0).T
        rows_out[...] = lines[0:8, :]
        loss_out[0, 0] = jnp.sum(lines[3:4, :])
        for step in range(1, 8):
            pieces(step).wait_recv()
            to_partner(step).start()
        for step in range(8):
            to_partner(step).wait_recv()
        for step in range(1, PIECES):
            scatter(step).wait_send()
        for step in range(1, CHIPS):
            across_heads(step).wait_send()
        for step in range(1, 8):
            pieces(step).wait_send()
        for step in range(8):
            to_partner(step).wait_send()

    hop2(0)
    hop2(1)
    hop3(0)

    def phase(i, carry):
        pl.when(i + 1 < CHUNKS)(lambda: hop3(i + 1))
        pl.when(i + 2 < CHUNKS)(lambda: hop2(i + 2))
        pl.when(i + FAR < CHUNKS)(lambda: hop1(i + FAR))

        @pl.when(i == 0)
        def _():
            for c in w_copies[1:]:
                c.wait()
            for c in w_remote:
                c.wait_recv()

        arrived(i)
        compute(i)
        return carry

    lax.fori_loop(0, CHUNKS, phase, 0)

    def send_late(i, carry):
        pl.when(i + lag >= CHUNKS)(lambda: send_out(i))
        return carry

    lax.fori_loop(0, CHUNKS, send_late, 0)
    packed = jnp.zeros((RATIO, L), f32)
    for n in range(4):
        line = jnp.sum(small[n * RATIO : (n + 1) * RATIO, :], axis=1, keepdims=True)
        packed = jnp.where(col_i[:RATIO] == n, line, packed)
    for r in range(PIECES):
        cols = slice(r * PIECE, (r + 1) * PIECE)
        mine[r, :, 0:PIECE] = gw[0:8, cols] + gw[8:16, cols]
        mine[r, :, PIECE:PACK] = packed
    sum_up()

    def finish(i, carry):
        for kind in range(11):
            hop(kind, i).wait_send()
        exchange(i).wait_send()
        target, far, _ = out_copy(i)
        pl.when(target != me)(lambda: far().wait_send())
        dst = out.at[:, pl.ds(pl.multiple_of(i * KB, KB), KB)]
        pltpu.make_async_copy(mixed.at[i], dst, o_rs.at[i]).wait()
        return carry

    lax.fori_loop(0, CHUNKS, finish, 0)
    for c in w_remote:
        c.wait_send()


def fused(order, bias, decay, gain, positions, hidden, qw, kvw, dtw):
    smem = pl.BlockSpec(memory_space=pltpu.SMEM)
    vmem = pl.BlockSpec(memory_space=pltpu.VMEM)
    hbm = pl.BlockSpec(memory_space=pl.ANY)
    dma = pltpu.SemaphoreType.DMA
    stacked = (RATIO * L, HD)
    return pl.pallas_call(
        body,
        out_shape=(
            jax.ShapeDtypeStruct((L, D), bf16),
            jax.ShapeDtypeStruct((QH, D), bf16),
            jax.ShapeDtypeStruct((8, L), f32),
            jax.ShapeDtypeStruct((1, 1), f32),
        ),
        in_specs=[smem, smem, smem, smem, vmem, vmem, hbm, hbm, hbm],
        out_specs=(hbm, vmem, vmem, smem),
        scratch_shapes=[
            pltpu.VMEM((PIECES, RATIO, PACK), f32),
            pltpu.VMEM((CHUNKS, CHIPS, L, KB), bf16),
            pltpu.VMEM((D, NW), bf16),
            pltpu.VMEM((CHUNKS, L, 512), bf16),
            pltpu.VMEM((RATIO, D), f32),
            pltpu.VMEM((32, D), bf16),
            pltpu.VMEM((L, NW), f32),
            pltpu.VMEM(stacked, bf16),
            pltpu.VMEM(stacked, bf16),
            pltpu.VMEM(stacked, f32),
            pltpu.VMEM(stacked, f32),
            pltpu.VMEM(stacked, f32),
            pltpu.VMEM(stacked, bf16),
            pltpu.VMEM((RATIO * L, 2 * HD), f32),
            pltpu.VMEM((16, D), f32),
            pltpu.VMEM((32, L), f32),
            pltpu.VMEM((CHUNKS, L, KB), bf16),
            dma((CHUNKS,)),
            dma((CHUNKS,)),
            dma((CHUNKS, 11)),
            dma((CHUNKS, 11)),
            dma((3,)),
            dma((2,)),
            dma((2,)),
            dma((CHUNKS,)),
            dma((CHIPS,)),
            pltpu.VMEM((PIECES, RATIO, PACK), f32),
            pltpu.VMEM((RATIO, PACK), f32),
            pltpu.VMEM((CHIPS, RATIO, PACK), f32),
            dma((PIECES,)),
            dma((PIECES,)),
            dma((CHIPS,)),
            dma((CHIPS,)),
            dma((8,)),
            dma((8,)),
            dma((8,)),
            dma((8,)),
        ],
        name="fused",
        compiler_params=pltpu.CompilerParams(
            collective_id=0, has_side_effects=True, vmem_limit_bytes=60 * 2**20
        ),
    )(order, bias, decay, gain, positions, hidden, qw, kvw, dtw)


def local(
    hidden_in,
    positions,
    assignment,
    query_weight,
    kv_weight,
    dt_weight,
    dt_bias,
    decay_log,
    skip_gain,
):
    student_out, narrow, rows, loss = fused(
        assignment,
        dt_bias,
        decay_log,
        skip_gain,
        positions.reshape(16, L),
        hidden_in.reshape(16, L, 512),
        query_weight,
        kv_weight,
        dt_weight.T,
    )
    grad = narrow.astype(f32)
    return student_out, grad.T, rows[0, :QH], rows[1, :QH], rows[2, :QH], loss.reshape(())


def solution(mesh):
    placed = (
        P("dp", "mp"),
        P("dp"),
        P("dp", None),
        P(None, "mp"),
        P(None, "mp"),
        P(),
        P(),
        P(),
        P(),
    )
    return jax.shard_map(
        local,
        mesh=mesh,
        in_specs=placed,
        out_specs=(P(("dp", "mp"), None), P(), P(), P(), P(), P()),
        check_vma=False,
    )
```

```python
import jax
import jax.numpy as jnp
from jax import lax
from jax.experimental import pallas as pl
from jax.experimental.pallas import tpu as pltpu
from jax.sharding import PartitionSpec as P

D = 8192
QH = 64
HD = 128
L = 128
RATIO = 8
CHUNKS = 8
CHIPS = 8
KB = 1024
TOTAL = 16384 * QH * HD
SCALE = HD**-0.5
KT = (384, 512)
NW = 1280
PIECES = 16
PIECE = D // PIECES
PACK = PIECE + L
FAR = 4
EARLY = 2
FIRST = 2
SECOND = 4
SHIFT = 4

highest = lax.Precision.HIGHEST
f32 = jnp.float32
bf16 = jnp.bfloat16


def dot_nt(a, b):
    return lax.dot_general(a, b, (((1,), (1,)), ((), ())), preferred_element_type=f32)


def dot_nn(a, b):
    return jnp.dot(a, b, preferred_element_type=f32)


def body(
    order,
    bias_s,
    decay_s,
    gain_s,
    positions,
    x_in,
    qw,
    kvw,
    dtw,
    out,
    narrow,
    rows_out,
    loss_out,
    mine,
    a_buf,
    w_buf,
    x_send,
    dt_stage,
    dt_parts,
    acc,
    qb,
    qt,
    s_t,
    s_s,
    n_buf,
    pb,
    o_buf,
    gw,
    small,
    mixed,
    ex_ss,
    ex_rs,
    g_ss,
    g_rs,
    w_sem,
    wr_ss,
    wr_rs,
    o_ss,
    o_rs,
    got,
    own,
    heads,
    s1s,
    s1r,
    s2s,
    s2r,
    s3s,
    s3r,
    s4s,
    s4r,
):
    me = lax.axis_index("mp")
    core = me % 2
    chip = me // 2
    x = chip // 4
    y = chip % 4
    xo = 1 - x
    up = (y + 1) % 4
    down = (y + 3) % 4
    across = (y + 2) % 4

    def device(xx, yy):
        return (xx * 4 + yy) * 2 + core

    def block(which, i):
        return which * CHUNKS + (i + SHIFT * which) % CHUNKS

    partner = chip * 2 + (1 - core)
    to_up, to_down, to_x = device(x, up), device(x, down), device(xo, y)

    d = lax.axis_index("dp")
    place = d * 2 + core

    def same_chip(step):
        r = (place + step) % PIECES
        return {"dp": r // 2, "mp": chip * 2 + r % 2}

    def same_core(step):
        return {"dp": d, "mp": (chip + step) % CHIPS * 2 + core}

    barrier = pltpu.get_barrier_semaphore()
    for step in range(1, 16):
        pl.semaphore_signal(barrier, inc=1, device_id={"dp": d, "mp": (me + step) % 16})
    for step in range(1, PIECES):
        pl.semaphore_signal(barrier, inc=1, device_id=same_chip(step))
    pl.semaphore_wait(barrier, 30)

    q_cols = pl.ds(pl.multiple_of(core * 512, 512), 512)
    kv_cols = pl.ds(pl.multiple_of(1024 + core * 128, 128), 128)

    def remote(src, dst, ss, rs, dev):
        return pltpu.make_async_remote_copy(
            src_ref=src, dst_ref=dst, send_sem=ss, recv_sem=rs, device_id={"mp": dev}
        )

    def stage(i, carry):
        a_buf[i, chip, :, q_cols] = x_in[order[0, block(core, i)]]
        x_send[i] = x_in[order[0, block(1 - core, i)]]
        return carry

    lax.fori_loop(0, CHUNKS, stage, 0)

    def exchange(i):
        return remote(x_send.at[i], a_buf.at[i, chip, :, q_cols], ex_ss.at[i], ex_rs.at[i], partner)

    def start_exchange(i, carry):
        exchange(i).start()
        return carry

    lax.fori_loop(0, CHUNKS, start_exchange, 0)

    w_copies = (
        pltpu.make_async_copy(
            dtw.at[pl.ds(pl.multiple_of(chip * RATIO, RATIO), RATIO), :], dt_stage, w_sem.at[2]
        ),
        pltpu.make_async_copy(qw, w_buf.at[:, q_cols], w_sem.at[0]),
        pltpu.make_async_copy(kvw, w_buf.at[:, kv_cols], w_sem.at[1]),
    )
    w_remote = (
        remote(qw, w_buf.at[:, q_cols], wr_ss.at[0], wr_rs.at[0], partner),
        remote(kvw, w_buf.at[:, kv_cols], wr_ss.at[1], wr_rs.at[1], partner),
    )

    every = pl.ds(0, L)
    whole = pl.ds(0, KB)

    low = pl.ds(0, L // 2)
    high = pl.ds(L // 2, L // 2)

    def hop(kind, i, kt):
        first = pl.ds(0, kt)
        second = pl.ds(kt, KB - kt)
        slot_x, slot_y, rows, cols, dev = (
            (x, y, every, whole, to_up),
            (x, y, every, whole, to_down),
            (x, y, every, whole, to_x),
            (x, down, every, second, to_up),
            (x, down, every, first, to_x),
            (x, up, high, first, to_down),
            (x, up, every, first, to_x),
            (xo, y, every, second, to_up),
            (xo, y, every, second, to_down),
            (x, across, every, first, to_x),
            (xo, up, every, second, to_down),
            (x, down, low, first, to_up),
        )[kind]
        ref = a_buf.at[i, slot_x * 4 + slot_y, rows, cols]
        return remote(ref, ref, g_ss.at[i, kind], g_rs.at[i, kind], dev)

    def hop1(i, kt):
        exchange(i).wait_recv()
        for kind in (0, 1, 2):
            hop(kind, i, kt).start()

    def hop2(i, kt):
        hop(0, i, kt).wait_recv()
        for kind in (3, 11, 4):
            hop(kind, i, kt).start()
        hop(1, i, kt).wait_recv()
        for kind in (5, 6):
            hop(kind, i, kt).start()
        hop(2, i, kt).wait_recv()
        for kind in (8, 7):
            hop(kind, i, kt).start()

    def hop3(i, kt):
        hop(8, i, kt).wait_recv()
        hop(10, i, kt).start()
        hop(5, i, kt).wait_recv()
        hop(11, i, kt).wait_recv()
        hop(9, i, kt).start()

    def arrived(i, kt):
        for kind in (3, 4, 6, 7, 9, 10):
            hop(kind, i, kt).wait_recv()

    def all_sent(i, kt):
        for kind in range(12):
            hop(kind, i, kt).wait_send()

    def in_turn(step, i):
        for odd in range(2):
            pl.when((i < CHUNKS) & (i % 2 == odd))(lambda: step(i, KT[odd]))

    for i in range(FAR):
        hop1(i, KT[i % 2])
    for c in w_copies:
        c.start()
    for c in w_remote:
        c.start()

    w_copies[0].wait()
    w = dt_stage[...]
    one = w.astype(bf16).astype(f32)
    two = (w - one).astype(bf16).astype(f32)
    three = w - one - two
    dt_parts[...] = jnp.concatenate([one, two, three, jnp.zeros_like(w)], axis=0).astype(bf16)
    gw[...] = jnp.zeros_like(gw)
    small[...] = jnp.zeros_like(small)

    row_i = lax.broadcasted_iota(jnp.int32, (L, L), 0)
    col_i = lax.broadcasted_iota(jnp.int32, (L, L), 1)
    causal = col_i <= row_i
    upper = jnp.where(row_i <= col_i, 1.0, 0.0).astype(f32)
    lower = jnp.where(row_i >= col_i, 1.0, 0.0).astype(f32)
    head_row = lax.broadcasted_iota(jnp.int32, (RATIO, L), 0)

    def per_head(ref):
        values = jnp.zeros((RATIO, L), f32)
        for h in range(RATIO):
            values = jnp.where(head_row == h, ref[chip * RATIO + h], values)
        return values

    def out_copy(i):
        dst = out.at[:, pl.ds(pl.multiple_of(chip * KB, KB), KB)]
        target = block(core, i)

        def far():
            return remote(mixed.at[i], dst, o_ss.at[i], o_rs.at[chip], target)

        def near():
            return pltpu.make_async_copy(mixed.at[i], dst, o_rs.at[chip])

        return target, far, near

    def send_out(i):
        target, far, near = out_copy(i)
        pl.when(target == me)(lambda: near().start())
        pl.when(target != me)(lambda: far().start())

    def compute(i):
        def project(n, carry):
            cols = pl.ds(pl.multiple_of(n * 256, 256), 256)
            total = dot_nn(a_buf[i, 0], w_buf[0:KB, cols])
            for m in range(1, CHIPS):
                total += dot_nn(a_buf[i, m], w_buf[m * KB : (m + 1) * KB, cols])
            acc[:, cols] = total
            return carry

        lax.fori_loop(0, NW // 256, project, 0)

        spots = positions[pl.ds(order[0, block(core, i)], 1), :].astype(f32)
        spots = jnp.broadcast_to(spots, (L, L)).T
        lane = col_i % (HD // 2)
        frequency = jnp.exp(lane.astype(f32) * f32(-2.0 / HD * 13.122363377404328))
        angle = spots * frequency
        cosine = jnp.cos(angle)
        sine = jnp.where(col_i < HD // 2, -jnp.sin(angle), jnp.sin(angle))

        def rotate(head):
            wide = head.astype(f32)
            return (wide * cosine + pltpu.roll(wide, HD // 2, 1) * sine).astype(bf16)

        k = acc[:, 1024:1152].astype(bf16)
        v = acc[:, 1152:1280].astype(bf16)
        v32 = v.astype(f32)
        k_turned = rotate(k)
        for h in range(RATIO):
            rows = pl.ds(h * L, L)
            q = acc[:, h * HD : (h + 1) * HD].astype(bf16)
            qb[rows, :] = q
            qt[rows, :] = rotate(q)
        s_t[...] = dot_nt(qt[...], k_turned)
        s_s[...] = dot_nt(qb[...], k)
        for h in range(RATIO):
            rows = pl.ds(h * L, L)
            scores = jnp.where(causal, s_t[rows, :] * SCALE, -jnp.inf)
            weights = jnp.exp(scores - jnp.max(scores, axis=1, keepdims=True))
            pb[rows, :] = weights.astype(bf16)
        o_buf[...] = dot_nn(pb[...], jnp.concatenate([v, jnp.ones_like(v)], axis=1))

        pre = dot_nt(dt_parts[:, 0:KB], a_buf[i, 0])
        for m in range(1, CHIPS):
            pre += dot_nt(dt_parts[:, m * KB : (m + 1) * KB], a_buf[i, m])
        raw = pre[0:8] + pre[8:16] + pre[16:24] + per_head(bias_s)
        step_size = jnp.maximum(raw, 0.0) + jnp.log1p(jnp.exp(-jnp.abs(raw)))
        rate = -jnp.exp(per_head(decay_s))
        summed = jnp.dot(step_size, upper, precision=highest, preferred_element_type=f32)
        level = rate * summed
        level_t = jnp.concatenate([level, jnp.zeros((L - RATIO, L), f32)], axis=0).T
        for h in range(RATIO):
            rows = pl.ds(h * L, L)
            spread = jnp.where(causal, level_t[:, h : h + 1] - level[h : h + 1, :], -jnp.inf)
            kept = s_s[rows, :] * SCALE * jnp.exp(spread)
            n_buf[rows, :] = kept
            pb[rows, :] = (kept * step_size[h : h + 1, :]).astype(bf16)
        s_s[...] = dot_nn(pb[...], v)
        gain_rows, loss_rows = [], []
        for h in range(RATIO):
            rows = pl.ds(h * L, L)
            teacher = o_buf[rows, :]
            target = (teacher[:, :HD] / teacher[:, HD:]).astype(bf16).astype(f32)
            value = s_s[rows, :] + gain_s[chip * RATIO + h] * v32
            mixed[i, :, h * HD : (h + 1) * HD] = value.astype(bf16)
            differ = value - target
            gain_rows.append(jnp.sum(differ * v32, axis=0, keepdims=True))
            loss_rows.append(jnp.sum(differ * differ, axis=0, keepdims=True))
            pb[rows, :] = differ.astype(bf16)

        @pl.when(i >= CHUNKS - EARLY)
        def _():
            send_out((chip + i) % EARLY)

        s_t[...] = dot_nt(pb[...], v)
        col_rows, row_cols = [], jnp.zeros((L, L), f32)
        for h in range(RATIO):
            rows = pl.ds(h * L, L)
            product = s_t[rows, :] * n_buf[rows, :]
            col_rows.append(jnp.sum(product, axis=0, keepdims=True))
            along = jnp.sum(product * step_size[h : h + 1, :], axis=1, keepdims=True)
            row_cols = jnp.where(col_i == h, along, row_cols)
        factor = f32(2.0 / TOTAL)
        by_col = jnp.concatenate(col_rows, axis=0) * factor
        by_row = row_cols.T[:RATIO, :] * factor
        d_level = by_row - step_size * by_col
        behind = jnp.dot(d_level, lower, precision=highest, preferred_element_type=f32)
        d_step = by_col + rate * behind
        d_raw = d_step * (1.0 / (1.0 + jnp.exp(-raw)))
        small[0:8, :] += d_raw
        small[8:16, :] += d_level * level
        small[16:24, :] += jnp.concatenate(gain_rows, axis=0) * factor
        small[24:32, :] += jnp.concatenate(loss_rows, axis=0) * f32(1.0 / TOTAL)
        upper_part = d_raw.astype(bf16).astype(f32)
        parts = jnp.concatenate([upper_part, d_raw - upper_part], axis=0).astype(bf16)
        for m in range(CHIPS):
            cols = slice(m * KB, (m + 1) * KB)
            gw[:, cols] += dot_nn(parts, a_buf[i, m])

    def scatter(step):
        return pltpu.make_async_remote_copy(
            src_ref=mine.at[(place + step) % PIECES],
            dst_ref=got.at[step],
            send_sem=s1s.at[step],
            recv_sem=s1r.at[step],
            device_id=same_chip(step),
        )

    def across_heads(step):
        return pltpu.make_async_remote_copy(
            src_ref=own,
            dst_ref=heads.at[chip],
            send_sem=s2s.at[step],
            recv_sem=s2r.at[step],
            device_id=same_core(step),
        )

    def columns(dd):
        at = (dd * 2 + core) * PIECE
        return narrow.at[:, pl.ds(pl.multiple_of(at, PIECE), PIECE)]

    def pieces(step):
        return pltpu.make_async_remote_copy(
            src_ref=columns(d),
            dst_ref=columns(d),
            send_sem=s3s.at[step],
            recv_sem=s3r.at[step],
            device_id={"dp": (d + step) % 8, "mp": me},
        )

    def to_partner(step):
        ref = columns((d + 8 - step) % 8)
        return remote(ref, ref, s4s.at[step], s4r.at[step], partner)

    def send_rest(begin, end):
        def send(i, carry):
            send_out(EARLY + (chip + i) % (CHUNKS - EARLY))
            return carry

        lax.fori_loop(begin, end, send, 0)

    def sum_up():
        for step in range(1, PIECES):
            scatter(step).start()
        send_rest(0, FIRST)
        total = mine[place]
        for step in range(1, PIECES):
            scatter(step).wait_recv()
            total += got[step]
        own[...] = total
        for step in range(1, CHIPS):
            across_heads(step).start()
        send_rest(FIRST, SECOND)
        heads[chip] = total
        for step in range(1, CHIPS):
            across_heads(step).wait_recv()
        at = pl.multiple_of(place * PIECE, PIECE)
        narrow[:, pl.ds(at, PIECE)] = heads[:, :, 0:PIECE].reshape(QH, PIECE).astype(bf16)
        for step in range(1, 8):
            pieces(step).start()
        to_partner(0).start()
        send_rest(SECOND, CHUNKS - EARLY)
        lines = heads[:, :, PIECE:PACK].reshape(QH, L)
        lines = jnp.concatenate([lines, jnp.zeros_like(lines)], axis=0).T
        rows_out[...] = lines[0:8, :]
        loss_out[0, 0] = jnp.sum(lines[3:4, :])
        for step in range(1, 8):
            pieces(step).wait_recv()
            to_partner(step).start()
        for step in range(8):
            to_partner(step).wait_recv()
        for step in range(1, PIECES):
            scatter(step).wait_send()
        for step in range(1, CHIPS):
            across_heads(step).wait_send()
        for step in range(1, 8):
            pieces(step).wait_send()
        for step in range(8):
            to_partner(step).wait_send()

    hop2(0, KT[0])
    hop2(1, KT[1])
    hop3(0, KT[0])

    def phase(i, carry):
        in_turn(hop3, i + 1)
        in_turn(hop2, i + 2)
        in_turn(hop1, i + FAR)

        @pl.when(i == 0)
        def _():
            for c in w_copies[1:]:
                c.wait()
            for c in w_remote:
                c.wait_recv()

        in_turn(arrived, i)
        compute(i)
        return carry

    lax.fori_loop(0, CHUNKS, phase, 0)

    packed = jnp.zeros((RATIO, L), f32)
    for n in range(4):
        line = jnp.sum(small[n * RATIO : (n + 1) * RATIO, :], axis=1, keepdims=True)
        packed = jnp.where(col_i[:RATIO] == n, line, packed)
    for r in range(PIECES):
        cols = slice(r * PIECE, (r + 1) * PIECE)
        mine[r, :, 0:PIECE] = gw[0:8, cols] + gw[8:16, cols]
        mine[r, :, PIECE:PACK] = packed
    sum_up()

    def finish(i, carry):
        in_turn(all_sent, i)
        exchange(i).wait_send()
        target, far, _ = out_copy(i)
        pl.when(target != me)(lambda: far().wait_send())
        dst = out.at[:, pl.ds(pl.multiple_of(i * KB, KB), KB)]
        pltpu.make_async_copy(mixed.at[i], dst, o_rs.at[i]).wait()
        return carry

    lax.fori_loop(0, CHUNKS, finish, 0)
    for c in w_remote:
        c.wait_send()


def fused(order, bias, decay, gain, positions, hidden, qw, kvw, dtw):
    smem = pl.BlockSpec(memory_space=pltpu.SMEM)
    vmem = pl.BlockSpec(memory_space=pltpu.VMEM)
    hbm = pl.BlockSpec(memory_space=pl.ANY)
    dma = pltpu.SemaphoreType.DMA
    stacked = (RATIO * L, HD)
    return pl.pallas_call(
        body,
        out_shape=(
            jax.ShapeDtypeStruct((L, D), bf16),
            jax.ShapeDtypeStruct((QH, D), bf16),
            jax.ShapeDtypeStruct((8, L), f32),
            jax.ShapeDtypeStruct((1, 1), f32),
        ),
        in_specs=[smem, smem, smem, smem, vmem, vmem, hbm, hbm, hbm],
        out_specs=(hbm, vmem, vmem, smem),
        scratch_shapes=[
            pltpu.VMEM((PIECES, RATIO, PACK), f32),
            pltpu.VMEM((CHUNKS, CHIPS, L, KB), bf16),
            pltpu.VMEM((D, NW), bf16),
            pltpu.VMEM((CHUNKS, L, 512), bf16),
            pltpu.VMEM((RATIO, D), f32),
            pltpu.VMEM((32, D), bf16),
            pltpu.VMEM((L, NW), f32),
            pltpu.VMEM(stacked, bf16),
            pltpu.VMEM(stacked, bf16),
            pltpu.VMEM(stacked, f32),
            pltpu.VMEM(stacked, f32),
            pltpu.VMEM(stacked, f32),
            pltpu.VMEM(stacked, bf16),
            pltpu.VMEM((RATIO * L, 2 * HD), f32),
            pltpu.VMEM((16, D), f32),
            pltpu.VMEM((32, L), f32),
            pltpu.VMEM((CHUNKS, L, KB), bf16),
            dma((CHUNKS,)),
            dma((CHUNKS,)),
            dma((CHUNKS, 12)),
            dma((CHUNKS, 12)),
            dma((3,)),
            dma((2,)),
            dma((2,)),
            dma((CHUNKS,)),
            dma((CHIPS,)),
            pltpu.VMEM((PIECES, RATIO, PACK), f32),
            pltpu.VMEM((RATIO, PACK), f32),
            pltpu.VMEM((CHIPS, RATIO, PACK), f32),
            dma((PIECES,)),
            dma((PIECES,)),
            dma((CHIPS,)),
            dma((CHIPS,)),
            dma((8,)),
            dma((8,)),
            dma((8,)),
            dma((8,)),
        ],
        name="fused",
        compiler_params=pltpu.CompilerParams(
            collective_id=0, has_side_effects=True, vmem_limit_bytes=60 * 2**20
        ),
    )(order, bias, decay, gain, positions, hidden, qw, kvw, dtw)


def local(
    hidden_in,
    positions,
    assignment,
    query_weight,
    kv_weight,
    dt_weight,
    dt_bias,
    decay_log,
    skip_gain,
):
    student_out, narrow, rows, loss = fused(
        assignment,
        dt_bias,
        decay_log,
        skip_gain,
        positions.reshape(16, L),
        hidden_in.reshape(16, L, 512),
        query_weight,
        kv_weight,
        dt_weight.T,
    )
    grad = narrow.astype(f32)
    return student_out, grad.T, rows[0, :QH], rows[1, :QH], rows[2, :QH], loss.reshape(())


def solution(mesh):
    placed = (
        P("dp", "mp"),
        P("dp"),
        P("dp", None),
        P(None, "mp"),
        P(None, "mp"),
        P(),
        P(),
        P(),
        P(),
    )
    return jax.shard_map(
        local,
        mesh=mesh,
        in_specs=placed,
        out_specs=(P(("dp", "mp"), None), P(), P(), P(), P(), P()),
        check_vma=False,
    )
```

```python
import jax
import jax.numpy as jnp
from jax import lax
from jax.experimental import pallas as pl
from jax.experimental.pallas import tpu as pltpu
from jax.sharding import PartitionSpec as P

D = 8192
QH = 64
HD = 128
L = 128
RATIO = 8
CHUNKS = 8
CHIPS = 8
KB = 1024
TOTAL = 16384 * QH * HD
SCALE = HD**-0.5
KT = (384, 512)
NW = 1280
PIECES = 16
PIECE = D // PIECES
PACK = PIECE + L
FAR = 4
EARLY = 4
FIRST = 1
SECOND = 2
SHIFT = 4

highest = lax.Precision.HIGHEST
f32 = jnp.float32
bf16 = jnp.bfloat16


def dot_nt(a, b):
    return lax.dot_general(a, b, (((1,), (1,)), ((), ())), preferred_element_type=f32)


def dot_nn(a, b):
    return jnp.dot(a, b, preferred_element_type=f32)


def body(
    order,
    bias_s,
    decay_s,
    gain_s,
    positions,
    x_in,
    qw,
    kvw,
    dtw,
    out,
    narrow,
    rows_out,
    loss_out,
    mine,
    a_buf,
    w_buf,
    x_send,
    dt_stage,
    dt_parts,
    acc,
    qb,
    qt,
    s_t,
    s_s,
    n_buf,
    pb,
    o_buf,
    gw,
    small,
    mixed,
    ex_ss,
    ex_rs,
    g_ss,
    g_rs,
    w_sem,
    wr_ss,
    wr_rs,
    o_ss,
    o_rs,
    got,
    own,
    heads,
    s1s,
    s1r,
    s2s,
    s2r,
    s3s,
    s3r,
    s4s,
    s4r,
):
    me = lax.axis_index("mp")
    core = me % 2
    chip = me // 2
    x = chip // 4
    y = chip % 4
    xo = 1 - x
    up = (y + 1) % 4
    down = (y + 3) % 4
    across = (y + 2) % 4

    def device(xx, yy):
        return (xx * 4 + yy) * 2 + core

    def block(which, i):
        return which * CHUNKS + (2 * i + 1 - which + (2 * which - 1) * (i // 4)) % CHUNKS

    partner = chip * 2 + (1 - core)
    to_up, to_down, to_x = device(x, up), device(x, down), device(xo, y)

    d = lax.axis_index("dp")
    place = d * 2 + core

    def same_chip(step):
        r = (place + step) % PIECES
        return {"dp": r // 2, "mp": chip * 2 + r % 2}

    def same_core(step):
        return {"dp": d, "mp": (chip + step) % CHIPS * 2 + core}

    barrier = pltpu.get_barrier_semaphore()
    for step in range(1, 16):
        pl.semaphore_signal(barrier, inc=1, device_id={"dp": d, "mp": (me + step) % 16})
    for step in range(1, PIECES):
        pl.semaphore_signal(barrier, inc=1, device_id=same_chip(step))
    pl.semaphore_wait(barrier, 30)

    q_cols = pl.ds(pl.multiple_of(core * 512, 512), 512)
    kv_cols = pl.ds(pl.multiple_of(1024 + core * 128, 128), 128)

    def remote(src, dst, ss, rs, dev):
        return pltpu.make_async_remote_copy(
            src_ref=src, dst_ref=dst, send_sem=ss, recv_sem=rs, device_id={"mp": dev}
        )

    def stage(i, carry):
        a_buf[i, chip, :, q_cols] = x_in[order[0, block(core, i)]]
        x_send[i] = x_in[order[0, block(1 - core, i)]]
        return carry

    lax.fori_loop(0, CHUNKS, stage, 0)

    def exchange(i):
        return remote(x_send.at[i], a_buf.at[i, chip, :, q_cols], ex_ss.at[i], ex_rs.at[i], partner)

    def start_exchange(i, carry):
        exchange(i).start()
        return carry

    lax.fori_loop(0, CHUNKS, start_exchange, 0)

    w_copies = (
        pltpu.make_async_copy(
            dtw.at[pl.ds(pl.multiple_of(chip * RATIO, RATIO), RATIO), :], dt_stage, w_sem.at[2]
        ),
        pltpu.make_async_copy(qw, w_buf.at[:, q_cols], w_sem.at[0]),
        pltpu.make_async_copy(kvw, w_buf.at[:, kv_cols], w_sem.at[1]),
    )
    w_remote = (
        remote(qw, w_buf.at[:, q_cols], wr_ss.at[0], wr_rs.at[0], partner),
        remote(kvw, w_buf.at[:, kv_cols], wr_ss.at[1], wr_rs.at[1], partner),
    )

    every = pl.ds(0, L)
    whole = pl.ds(0, KB)

    low = pl.ds(0, L // 2)
    high = pl.ds(L // 2, L // 2)

    def hop(kind, i, kt):
        first = pl.ds(0, kt)
        second = pl.ds(kt, KB - kt)
        slot_x, slot_y, rows, cols, dev = (
            (x, y, every, whole, to_up),
            (x, y, every, whole, to_down),
            (x, y, every, whole, to_x),
            (x, down, every, second, to_up),
            (x, down, every, first, to_x),
            (x, up, high, first, to_down),
            (x, up, every, first, to_x),
            (xo, y, every, second, to_up),
            (xo, y, every, second, to_down),
            (x, across, every, first, to_x),
            (xo, up, every, second, to_down),
            (x, down, low, first, to_up),
        )[kind]
        ref = a_buf.at[i, slot_x * 4 + slot_y, rows, cols]
        return remote(ref, ref, g_ss.at[i, kind], g_rs.at[i, kind], dev)

    def hop1(i, kt):
        exchange(i).wait_recv()
        for kind in (0, 1, 2):
            hop(kind, i, kt).start()

    def hop2(i, kt):
        hop(0, i, kt).wait_recv()
        for kind in (3, 11, 4):
            hop(kind, i, kt).start()
        hop(1, i, kt).wait_recv()
        for kind in (5, 6):
            hop(kind, i, kt).start()
        hop(2, i, kt).wait_recv()
        for kind in (8, 7):
            hop(kind, i, kt).start()

    def hop3(i, kt):
        hop(8, i, kt).wait_recv()
        hop(10, i, kt).start()
        hop(5, i, kt).wait_recv()
        hop(11, i, kt).wait_recv()
        hop(9, i, kt).start()

    def arrived(i, kt):
        for kind in (3, 4, 6, 7, 9, 10):
            hop(kind, i, kt).wait_recv()

    def all_sent(i, kt):
        for kind in range(12):
            hop(kind, i, kt).wait_send()

    def in_turn(step, i):
        for odd in range(2):
            pl.when((i < CHUNKS) & (i % 2 == odd))(lambda: step(i, KT[odd]))

    for i in range(FAR):
        hop1(i, KT[i % 2])
    for c in w_copies:
        c.start()
    for c in w_remote:
        c.start()

    w_copies[0].wait()
    w = dt_stage[...]
    one = w.astype(bf16).astype(f32)
    two = (w - one).astype(bf16).astype(f32)
    three = w - one - two
    dt_parts[...] = jnp.concatenate([one, two, three, jnp.zeros_like(w)], axis=0).astype(bf16)
    gw[...] = jnp.zeros_like(gw)
    small[...] = jnp.zeros_like(small)

    row_i = lax.broadcasted_iota(jnp.int32, (L, L), 0)
    col_i = lax.broadcasted_iota(jnp.int32, (L, L), 1)
    causal = col_i <= row_i
    upper = jnp.where(row_i <= col_i, 1.0, 0.0).astype(f32)
    lower = jnp.where(row_i >= col_i, 1.0, 0.0).astype(f32)
    head_row = lax.broadcasted_iota(jnp.int32, (RATIO, L), 0)

    def per_head(ref):
        values = jnp.zeros((RATIO, L), f32)
        for h in range(RATIO):
            values = jnp.where(head_row == h, ref[chip * RATIO + h], values)
        return values

    def out_copy(i):
        dst = out.at[:, pl.ds(pl.multiple_of(chip * KB, KB), KB)]
        target = block(core, i)

        def far():
            return remote(mixed.at[i], dst, o_ss.at[i], o_rs.at[chip], target)

        def near():
            return pltpu.make_async_copy(mixed.at[i], dst, o_rs.at[chip])

        return target, far, near

    def send_out(i):
        target, far, near = out_copy(i)
        pl.when(target == me)(lambda: near().start())
        pl.when(target != me)(lambda: far().start())

    def compute(i):
        def project(n, carry):
            cols = pl.ds(pl.multiple_of(n * 256, 256), 256)
            total = dot_nn(a_buf[i, 0], w_buf[0:KB, cols])
            for m in range(1, CHIPS):
                total += dot_nn(a_buf[i, m], w_buf[m * KB : (m + 1) * KB, cols])
            acc[:, cols] = total
            return carry

        lax.fori_loop(0, NW // 256, project, 0)

        spots = positions[pl.ds(order[0, block(core, i)], 1), :].astype(f32)
        spots = jnp.broadcast_to(spots, (L, L)).T
        lane = col_i % (HD // 2)
        frequency = jnp.exp(lane.astype(f32) * f32(-2.0 / HD * 13.122363377404328))
        angle = spots * frequency
        cosine = jnp.cos(angle)
        sine = jnp.where(col_i < HD // 2, -jnp.sin(angle), jnp.sin(angle))

        def rotate(head):
            wide = head.astype(f32)
            return (wide * cosine + pltpu.roll(wide, HD // 2, 1) * sine).astype(bf16)

        k = acc[:, 1024:1152].astype(bf16)
        v = acc[:, 1152:1280].astype(bf16)
        v32 = v.astype(f32)
        k_turned = rotate(k)
        for h in range(RATIO):
            rows = pl.ds(h * L, L)
            q = acc[:, h * HD : (h + 1) * HD].astype(bf16)
            qb[rows, :] = q
            qt[rows, :] = rotate(q)
        s_t[...] = dot_nt(qt[...], k_turned)
        s_s[...] = dot_nt(qb[...], k)
        for h in range(RATIO):
            rows = pl.ds(h * L, L)
            scores = jnp.where(causal, s_t[rows, :] * SCALE, -jnp.inf)
            weights = jnp.exp(scores - jnp.max(scores, axis=1, keepdims=True))
            pb[rows, :] = weights.astype(bf16)
        o_buf[...] = dot_nn(pb[...], jnp.concatenate([v, jnp.ones_like(v)], axis=1))

        pre = dot_nt(dt_parts[:, 0:KB], a_buf[i, 0])
        for m in range(1, CHIPS):
            pre += dot_nt(dt_parts[:, m * KB : (m + 1) * KB], a_buf[i, m])
        raw = pre[0:8] + pre[8:16] + pre[16:24] + per_head(bias_s)
        step_size = jnp.maximum(raw, 0.0) + jnp.log1p(jnp.exp(-jnp.abs(raw)))
        rate = -jnp.exp(per_head(decay_s))
        summed = jnp.dot(step_size, upper, precision=highest, preferred_element_type=f32)
        level = rate * summed
        level_t = jnp.concatenate([level, jnp.zeros((L - RATIO, L), f32)], axis=0).T
        for h in range(RATIO):
            rows = pl.ds(h * L, L)
            spread = jnp.where(causal, level_t[:, h : h + 1] - level[h : h + 1, :], -jnp.inf)
            kept = s_s[rows, :] * SCALE * jnp.exp(spread)
            n_buf[rows, :] = kept
            pb[rows, :] = (kept * step_size[h : h + 1, :]).astype(bf16)
        s_s[...] = dot_nn(pb[...], v)
        gain_rows, loss_rows = [], []
        for h in range(RATIO):
            rows = pl.ds(h * L, L)
            teacher = o_buf[rows, :]
            target = (teacher[:, :HD] / teacher[:, HD:]).astype(bf16).astype(f32)
            value = s_s[rows, :] + gain_s[chip * RATIO + h] * v32
            mixed[i, :, h * HD : (h + 1) * HD] = value.astype(bf16)
            differ = value - target
            gain_rows.append(jnp.sum(differ * v32, axis=0, keepdims=True))
            loss_rows.append(jnp.sum(differ * differ, axis=0, keepdims=True))
            pb[rows, :] = differ.astype(bf16)

        s_t[...] = dot_nt(pb[...], v)
        col_rows, row_cols = [], jnp.zeros((L, L), f32)
        for h in range(RATIO):
            rows = pl.ds(h * L, L)
            product = s_t[rows, :] * n_buf[rows, :]
            col_rows.append(jnp.sum(product, axis=0, keepdims=True))
            along = jnp.sum(product * step_size[h : h + 1, :], axis=1, keepdims=True)
            row_cols = jnp.where(col_i == h, along, row_cols)
        factor = f32(2.0 / TOTAL)
        by_col = jnp.concatenate(col_rows, axis=0) * factor
        by_row = row_cols.T[:RATIO, :] * factor
        d_level = by_row - step_size * by_col
        behind = jnp.dot(d_level, lower, precision=highest, preferred_element_type=f32)
        d_step = by_col + rate * behind
        d_raw = d_step * (1.0 / (1.0 + jnp.exp(-raw)))
        small[0:8, :] += d_raw
        small[8:16, :] += d_level * level
        small[16:24, :] += jnp.concatenate(gain_rows, axis=0) * factor
        small[24:32, :] += jnp.concatenate(loss_rows, axis=0) * f32(1.0 / TOTAL)
        upper_part = d_raw.astype(bf16).astype(f32)
        parts = jnp.concatenate([upper_part, d_raw - upper_part], axis=0).astype(bf16)
        for m in range(CHIPS):
            cols = slice(m * KB, (m + 1) * KB)
            gw[:, cols] += dot_nn(parts, a_buf[i, m])

    def scatter(step):
        return pltpu.make_async_remote_copy(
            src_ref=mine.at[(place + step) % PIECES],
            dst_ref=got.at[step],
            send_sem=s1s.at[step],
            recv_sem=s1r.at[step],
            device_id=same_chip(step),
        )

    def across_heads(step):
        return pltpu.make_async_remote_copy(
            src_ref=own,
            dst_ref=heads.at[chip],
            send_sem=s2s.at[step],
            recv_sem=s2r.at[step],
            device_id=same_core(step),
        )

    def columns(dd):
        at = (dd * 2 + core) * PIECE
        return narrow.at[:, pl.ds(pl.multiple_of(at, PIECE), PIECE)]

    def pieces(step):
        return pltpu.make_async_remote_copy(
            src_ref=columns(d),
            dst_ref=columns(d),
            send_sem=s3s.at[step],
            recv_sem=s3r.at[step],
            device_id={"dp": (d + step) % 8, "mp": me},
        )

    def to_partner(step):
        ref = columns((d + 8 - step) % 8)
        return remote(ref, ref, s4s.at[step], s4r.at[step], partner)

    def send_rest(begin, end):
        def send(i, carry):
            send_out(EARLY + (chip + i) % (CHUNKS - EARLY))
            return carry

        lax.fori_loop(begin, end, send, 0)

    def sum_up():
        for step in range(1, PIECES):
            scatter(step).start()
        send_rest(0, FIRST)
        total = mine[place]
        for step in range(1, PIECES):
            scatter(step).wait_recv()
            total += got[step]
        own[...] = total
        for step in range(1, CHIPS):
            across_heads(step).start()
        send_rest(FIRST, SECOND)
        heads[chip] = total
        for step in range(1, CHIPS):
            across_heads(step).wait_recv()
        at = pl.multiple_of(place * PIECE, PIECE)
        narrow[:, pl.ds(at, PIECE)] = heads[:, :, 0:PIECE].reshape(QH, PIECE).astype(bf16)
        for step in range(1, 8):
            pieces(step).start()
        to_partner(0).start()
        send_rest(SECOND, CHUNKS - EARLY)
        lines = heads[:, :, PIECE:PACK].reshape(QH, L)
        lines = jnp.concatenate([lines, jnp.zeros_like(lines)], axis=0).T
        rows_out[...] = lines[0:8, :]
        loss_out[0, 0] = jnp.sum(lines[3:4, :])
        for step in range(1, 8):
            pieces(step).wait_recv()
            to_partner(step).start()
        for step in range(8):
            to_partner(step).wait_recv()
        for step in range(1, PIECES):
            scatter(step).wait_send()
        for step in range(1, CHIPS):
            across_heads(step).wait_send()
        for step in range(1, 8):
            pieces(step).wait_send()
        for step in range(8):
            to_partner(step).wait_send()

    hop2(0, KT[0])
    hop2(1, KT[1])
    hop3(0, KT[0])

    def phase(i, carry):
        in_turn(hop3, i + 1)
        in_turn(hop2, i + 2)
        in_turn(hop1, i + FAR)

        @pl.when(i == 0)
        def _():
            for c in w_copies[1:]:
                c.wait()
            for c in w_remote:
                c.wait_recv()

        in_turn(arrived, i)

        @pl.when(i >= CHUNKS - EARLY // 2)
        def _():
            for n in range(2):
                send_out((i - (CHUNKS - EARLY // 2)) * 2 + (chip + n) % 2)

        compute(i)
        return carry

    lax.fori_loop(0, CHUNKS, phase, 0)

    packed = jnp.zeros((RATIO, L), f32)
    for n in range(4):
        line = jnp.sum(small[n * RATIO : (n + 1) * RATIO, :], axis=1, keepdims=True)
        packed = jnp.where(col_i[:RATIO] == n, line, packed)
    for r in range(PIECES):
        cols = slice(r * PIECE, (r + 1) * PIECE)
        mine[r, :, 0:PIECE] = gw[0:8, cols] + gw[8:16, cols]
        mine[r, :, PIECE:PACK] = packed
    sum_up()

    def finish(i, carry):
        in_turn(all_sent, i)
        exchange(i).wait_send()
        target, far, _ = out_copy(i)
        pl.when(target != me)(lambda: far().wait_send())
        dst = out.at[:, pl.ds(pl.multiple_of(i * KB, KB), KB)]
        pltpu.make_async_copy(mixed.at[i], dst, o_rs.at[i]).wait()
        return carry

    lax.fori_loop(0, CHUNKS, finish, 0)
    for c in w_remote:
        c.wait_send()


def fused(order, bias, decay, gain, positions, hidden, qw, kvw, dtw):
    smem = pl.BlockSpec(memory_space=pltpu.SMEM)
    vmem = pl.BlockSpec(memory_space=pltpu.VMEM)
    hbm = pl.BlockSpec(memory_space=pl.ANY)
    dma = pltpu.SemaphoreType.DMA
    stacked = (RATIO * L, HD)
    return pl.pallas_call(
        body,
        out_shape=(
            jax.ShapeDtypeStruct((L, D), bf16),
            jax.ShapeDtypeStruct((QH, D), bf16),
            jax.ShapeDtypeStruct((8, L), f32),
            jax.ShapeDtypeStruct((1, 1), f32),
        ),
        in_specs=[smem, smem, smem, smem, vmem, vmem, hbm, hbm, hbm],
        out_specs=(hbm, vmem, vmem, smem),
        scratch_shapes=[
            pltpu.VMEM((PIECES, RATIO, PACK), f32),
            pltpu.VMEM((CHUNKS, CHIPS, L, KB), bf16),
            pltpu.VMEM((D, NW), bf16),
            pltpu.VMEM((CHUNKS, L, 512), bf16),
            pltpu.VMEM((RATIO, D), f32),
            pltpu.VMEM((32, D), bf16),
            pltpu.VMEM((L, NW), f32),
            pltpu.VMEM(stacked, bf16),
            pltpu.VMEM(stacked, bf16),
            pltpu.VMEM(stacked, f32),
            pltpu.VMEM(stacked, f32),
            pltpu.VMEM(stacked, f32),
            pltpu.VMEM(stacked, bf16),
            pltpu.VMEM((RATIO * L, 2 * HD), f32),
            pltpu.VMEM((16, D), f32),
            pltpu.VMEM((32, L), f32),
            pltpu.VMEM((CHUNKS, L, KB), bf16),
            dma((CHUNKS,)),
            dma((CHUNKS,)),
            dma((CHUNKS, 12)),
            dma((CHUNKS, 12)),
            dma((3,)),
            dma((2,)),
            dma((2,)),
            dma((CHUNKS,)),
            dma((CHIPS,)),
            pltpu.VMEM((PIECES, RATIO, PACK), f32),
            pltpu.VMEM((RATIO, PACK), f32),
            pltpu.VMEM((CHIPS, RATIO, PACK), f32),
            dma((PIECES,)),
            dma((PIECES,)),
            dma((CHIPS,)),
            dma((CHIPS,)),
            dma((8,)),
            dma((8,)),
            dma((8,)),
            dma((8,)),
        ],
        name="fused",
        compiler_params=pltpu.CompilerParams(
            collective_id=0, has_side_effects=True, vmem_limit_bytes=60 * 2**20
        ),
    )(order, bias, decay, gain, positions, hidden, qw, kvw, dtw)


def local(
    hidden_in,
    positions,
    assignment,
    query_weight,
    kv_weight,
    dt_weight,
    dt_bias,
    decay_log,
    skip_gain,
):
    student_out, narrow, rows, loss = fused(
        assignment,
        dt_bias,
        decay_log,
        skip_gain,
        positions.reshape(16, L),
        hidden_in.reshape(16, L, 512),
        query_weight,
        kv_weight,
        dt_weight.T,
    )
    grad = narrow.astype(f32)
    return student_out, grad.T, rows[0, :QH], rows[1, :QH], rows[2, :QH], loss.reshape(())


def solution(mesh):
    placed = (
        P("dp", "mp"),
        P("dp"),
        P("dp", None),
        P(None, "mp"),
        P(None, "mp"),
        P(),
        P(),
        P(),
        P(),
    )
    return jax.shard_map(
        local,
        mesh=mesh,
        in_specs=placed,
        out_specs=(P(("dp", "mp"), None), P(), P(), P(), P(), P()),
        check_vma=False,
    )
```

```python
import jax
import jax.numpy as jnp
from jax import lax
from jax.experimental import pallas as pl
from jax.experimental.pallas import tpu as pltpu
from jax.sharding import PartitionSpec as P

D = 8192
QH = 64
HD = 128
L = 128
RATIO = 8
CHUNKS = 8
CHIPS = 8
KB = 1024
TOTAL = 16384 * QH * HD
SCALE = HD**-0.5
KT = (384, 512)
NW = 1280
PIECES = 16
PIECE = D // PIECES
PACK = PIECE + L
FAR = 4
EARLY = 4
FIRST = 1
SECOND = 2
SHIFT = 4

highest = lax.Precision.HIGHEST
f32 = jnp.float32
bf16 = jnp.bfloat16


def dot_nt(a, b):
    return lax.dot_general(a, b, (((1,), (1,)), ((), ())), preferred_element_type=f32)


def dot_nn(a, b):
    return jnp.dot(a, b, preferred_element_type=f32)


def body(
    order,
    bias_s,
    decay_s,
    gain_s,
    positions,
    x_in,
    qw,
    kvw,
    dtw,
    out,
    narrow,
    rows_out,
    loss_out,
    mine,
    a_buf,
    w_buf,
    x_send,
    dt_stage,
    dt_parts,
    acc,
    qb,
    qt,
    s_t,
    s_s,
    n_buf,
    pb,
    o_buf,
    gw,
    small,
    mixed,
    ex_ss,
    ex_rs,
    g_ss,
    g_rs,
    w_sem,
    wr_ss,
    wr_rs,
    o_ss,
    o_rs,
    got,
    own,
    heads,
    s1s,
    s1r,
    s2s,
    s2r,
    s3s,
    s3r,
    s4s,
    s4r,
):
    me = lax.axis_index("mp")
    core = me % 2
    chip = me // 2
    x = chip // 4
    y = chip % 4
    xo = 1 - x
    up = (y + 1) % 4
    down = (y + 3) % 4
    across = (y + 2) % 4

    def device(xx, yy):
        return (xx * 4 + yy) * 2 + core

    def block(which, i):
        return which * CHUNKS + (2 * i + 1 - which + (2 * which - 1) * (i // 4)) % CHUNKS

    partner = chip * 2 + (1 - core)
    to_up, to_down, to_x = device(x, up), device(x, down), device(xo, y)

    d = lax.axis_index("dp")
    place = d * 2 + core

    def same_chip(step):
        r = (place + step) % PIECES
        return {"dp": r // 2, "mp": chip * 2 + r % 2}

    def same_core(step):
        return {"dp": d, "mp": (chip + step) % CHIPS * 2 + core}

    barrier = pltpu.get_barrier_semaphore()
    for step in range(1, 16):
        pl.semaphore_signal(barrier, inc=1, device_id={"dp": d, "mp": (me + step) % 16})
    for step in range(1, PIECES):
        pl.semaphore_signal(barrier, inc=1, device_id=same_chip(step))
    pl.semaphore_wait(barrier, 30)

    q_cols = pl.ds(pl.multiple_of(core * 512, 512), 512)
    kv_cols = pl.ds(pl.multiple_of(1024 + core * 128, 128), 128)

    def remote(src, dst, ss, rs, dev):
        return pltpu.make_async_remote_copy(
            src_ref=src, dst_ref=dst, send_sem=ss, recv_sem=rs, device_id={"mp": dev}
        )

    def exchange(i):
        return remote(x_send.at[i], a_buf.at[i, chip, :, q_cols], ex_ss.at[i], ex_rs.at[i], partner)

    def stage(i, carry):
        x_send[i] = x_in[order[0, block(1 - core, i)]]
        exchange(i).start()
        a_buf[i, chip, :, q_cols] = x_in[order[0, block(core, i)]]
        return carry

    lax.fori_loop(0, FAR, stage, 0)

    w_copies = (
        pltpu.make_async_copy(
            dtw.at[pl.ds(pl.multiple_of(chip * RATIO, RATIO), RATIO), :], dt_stage, w_sem.at[2]
        ),
        pltpu.make_async_copy(qw, w_buf.at[:, q_cols], w_sem.at[0]),
        pltpu.make_async_copy(kvw, w_buf.at[:, kv_cols], w_sem.at[1]),
    )
    w_remote = (
        remote(qw, w_buf.at[:, q_cols], wr_ss.at[0], wr_rs.at[0], partner),
        remote(kvw, w_buf.at[:, kv_cols], wr_ss.at[1], wr_rs.at[1], partner),
    )

    every = pl.ds(0, L)
    whole = pl.ds(0, KB)

    low = pl.ds(0, L // 2)
    high = pl.ds(L // 2, L // 2)

    def hop(kind, i, kt):
        first = pl.ds(0, kt)
        second = pl.ds(kt, KB - kt)
        slot_x, slot_y, rows, cols, dev = (
            (x, y, every, whole, to_up),
            (x, y, every, whole, to_down),
            (x, y, every, whole, to_x),
            (x, down, every, second, to_up),
            (x, down, every, first, to_x),
            (x, up, high, first, to_down),
            (x, up, every, first, to_x),
            (xo, y, every, second, to_up),
            (xo, y, every, second, to_down),
            (x, across, every, first, to_x),
            (xo, up, every, second, to_down),
            (x, down, low, first, to_up),
        )[kind]
        ref = a_buf.at[i, slot_x * 4 + slot_y, rows, cols]
        return remote(ref, ref, g_ss.at[i, kind], g_rs.at[i, kind], dev)

    def hop1(i, kt):
        exchange(i).wait_recv()
        for kind in (0, 1, 2):
            hop(kind, i, kt).start()

    def hop2(i, kt):
        hop(0, i, kt).wait_recv()
        for kind in (3, 11, 4):
            hop(kind, i, kt).start()
        hop(1, i, kt).wait_recv()
        for kind in (5, 6):
            hop(kind, i, kt).start()
        hop(2, i, kt).wait_recv()
        for kind in (8, 7):
            hop(kind, i, kt).start()

    def hop3(i, kt):
        hop(8, i, kt).wait_recv()
        hop(10, i, kt).start()
        hop(5, i, kt).wait_recv()
        hop(11, i, kt).wait_recv()
        hop(9, i, kt).start()

    def arrived(i, kt):
        for kind in (3, 4, 6, 7, 9, 10):
            hop(kind, i, kt).wait_recv()

    def all_sent(i, kt):
        for kind in range(12):
            hop(kind, i, kt).wait_send()

    def in_turn(step, i):
        for odd in range(2):
            pl.when((i < CHUNKS) & (i % 2 == odd))(lambda: step(i, KT[odd]))

    for i in range(FAR):
        hop1(i, KT[i % 2])
    lax.fori_loop(FAR, CHUNKS, stage, 0)
    for c in w_copies:
        c.start()
    for c in w_remote:
        c.start()

    w_copies[0].wait()
    w = dt_stage[...]
    one = w.astype(bf16).astype(f32)
    two = (w - one).astype(bf16).astype(f32)
    three = w - one - two
    dt_parts[...] = jnp.concatenate([one, two, three, jnp.zeros_like(w)], axis=0).astype(bf16)
    gw[...] = jnp.zeros_like(gw)
    small[...] = jnp.zeros_like(small)

    row_i = lax.broadcasted_iota(jnp.int32, (L, L), 0)
    col_i = lax.broadcasted_iota(jnp.int32, (L, L), 1)
    causal = col_i <= row_i
    upper = jnp.where(row_i <= col_i, 1.0, 0.0).astype(f32)
    lower = jnp.where(row_i >= col_i, 1.0, 0.0).astype(f32)
    head_row = lax.broadcasted_iota(jnp.int32, (RATIO, L), 0)

    def per_head(ref):
        values = jnp.zeros((RATIO, L), f32)
        for h in range(RATIO):
            values = jnp.where(head_row == h, ref[chip * RATIO + h], values)
        return values

    def out_copy(i):
        dst = out.at[:, pl.ds(pl.multiple_of(chip * KB, KB), KB)]
        target = block(core, i)

        def far():
            return remote(mixed.at[i], dst, o_ss.at[i], o_rs.at[chip], target)

        def near():
            return pltpu.make_async_copy(mixed.at[i], dst, o_rs.at[chip])

        return target, far, near

    def send_out(i):
        target, far, near = out_copy(i)
        pl.when(target == me)(lambda: near().start())
        pl.when(target != me)(lambda: far().start())

    def compute(i):
        def project(n, carry):
            cols = pl.ds(pl.multiple_of(n * 256, 256), 256)
            total = dot_nn(a_buf[i, 0], w_buf[0:KB, cols])
            for m in range(1, CHIPS):
                total += dot_nn(a_buf[i, m], w_buf[m * KB : (m + 1) * KB, cols])
            acc[:, cols] = total
            return carry

        lax.fori_loop(0, NW // 256, project, 0)

        spots = positions[pl.ds(order[0, block(core, i)], 1), :].astype(f32)
        spots = jnp.broadcast_to(spots, (L, L)).T
        lane = col_i % (HD // 2)
        frequency = jnp.exp(lane.astype(f32) * f32(-2.0 / HD * 13.122363377404328))
        angle = spots * frequency
        cosine = jnp.cos(angle)
        sine = jnp.where(col_i < HD // 2, -jnp.sin(angle), jnp.sin(angle))

        def rotate(head):
            wide = head.astype(f32)
            return (wide * cosine + pltpu.roll(wide, HD // 2, 1) * sine).astype(bf16)

        k = acc[:, 1024:1152].astype(bf16)
        v = acc[:, 1152:1280].astype(bf16)
        v32 = v.astype(f32)
        k_turned = rotate(k)
        for h in range(RATIO):
            rows = pl.ds(h * L, L)
            q = acc[:, h * HD : (h + 1) * HD].astype(bf16)
            qb[rows, :] = q
            qt[rows, :] = rotate(q)
        s_t[...] = dot_nt(qt[...], k_turned)
        s_s[...] = dot_nt(qb[...], k)
        for h in range(RATIO):
            rows = pl.ds(h * L, L)
            scores = jnp.where(causal, s_t[rows, :] * SCALE, -jnp.inf)
            weights = jnp.exp(scores - jnp.max(scores, axis=1, keepdims=True))
            pb[rows, :] = weights.astype(bf16)
        o_buf[...] = dot_nn(pb[...], jnp.concatenate([v, jnp.ones_like(v)], axis=1))

        pre = dot_nt(dt_parts[:, 0:KB], a_buf[i, 0])
        for m in range(1, CHIPS):
            pre += dot_nt(dt_parts[:, m * KB : (m + 1) * KB], a_buf[i, m])
        raw = pre[0:8] + pre[8:16] + pre[16:24] + per_head(bias_s)
        step_size = jnp.maximum(raw, 0.0) + jnp.log1p(jnp.exp(-jnp.abs(raw)))
        rate = -jnp.exp(per_head(decay_s))
        summed = jnp.dot(step_size, upper, precision=highest, preferred_element_type=f32)
        level = rate * summed
        level_t = jnp.concatenate([level, jnp.zeros((L - RATIO, L), f32)], axis=0).T
        for h in range(RATIO):
            rows = pl.ds(h * L, L)
            spread = jnp.where(causal, level_t[:, h : h + 1] - level[h : h + 1, :], -jnp.inf)
            kept = s_s[rows, :] * SCALE * jnp.exp(spread)
            n_buf[rows, :] = kept
            pb[rows, :] = (kept * step_size[h : h + 1, :]).astype(bf16)
        s_s[...] = dot_nn(pb[...], v)
        gain_rows, loss_rows = [], []
        for h in range(RATIO):
            rows = pl.ds(h * L, L)
            teacher = o_buf[rows, :]
            target = (teacher[:, :HD] / teacher[:, HD:]).astype(bf16).astype(f32)
            value = s_s[rows, :] + gain_s[chip * RATIO + h] * v32
            mixed[i, :, h * HD : (h + 1) * HD] = value.astype(bf16)
            differ = value - target
            gain_rows.append(jnp.sum(differ * v32, axis=0, keepdims=True))
            loss_rows.append(jnp.sum(differ * differ, axis=0, keepdims=True))
            pb[rows, :] = differ.astype(bf16)

        s_t[...] = dot_nt(pb[...], v)
        col_rows, row_cols = [], jnp.zeros((L, L), f32)
        for h in range(RATIO):
            rows = pl.ds(h * L, L)
            product = s_t[rows, :] * n_buf[rows, :]
            col_rows.append(jnp.sum(product, axis=0, keepdims=True))
            along = jnp.sum(product * step_size[h : h + 1, :], axis=1, keepdims=True)
            row_cols = jnp.where(col_i == h, along, row_cols)
        factor = f32(2.0 / TOTAL)
        by_col = jnp.concatenate(col_rows, axis=0) * factor
        by_row = row_cols.T[:RATIO, :] * factor
        d_level = by_row - step_size * by_col
        behind = jnp.dot(d_level, lower, precision=highest, preferred_element_type=f32)
        d_step = by_col + rate * behind
        d_raw = d_step * (1.0 / (1.0 + jnp.exp(-raw)))
        small[0:8, :] += d_raw
        small[8:16, :] += d_level * level
        small[16:24, :] += jnp.concatenate(gain_rows, axis=0) * factor
        small[24:32, :] += jnp.concatenate(loss_rows, axis=0) * f32(1.0 / TOTAL)
        upper_part = d_raw.astype(bf16).astype(f32)
        parts = jnp.concatenate([upper_part, d_raw - upper_part], axis=0).astype(bf16)
        for m in range(CHIPS):
            cols = slice(m * KB, (m + 1) * KB)
            gw[:, cols] += dot_nn(parts, a_buf[i, m])

    def scatter(step):
        return pltpu.make_async_remote_copy(
            src_ref=mine.at[(place + step) % PIECES],
            dst_ref=got.at[step],
            send_sem=s1s.at[step],
            recv_sem=s1r.at[step],
            device_id=same_chip(step),
        )

    def across_heads(step):
        return pltpu.make_async_remote_copy(
            src_ref=own,
            dst_ref=heads.at[chip],
            send_sem=s2s.at[step],
            recv_sem=s2r.at[step],
            device_id=same_core(step),
        )

    def columns(dd):
        at = (dd * 2 + core) * PIECE
        return narrow.at[:, pl.ds(pl.multiple_of(at, PIECE), PIECE)]

    def pieces(step):
        return pltpu.make_async_remote_copy(
            src_ref=columns(d),
            dst_ref=columns(d),
            send_sem=s3s.at[step],
            recv_sem=s3r.at[step],
            device_id={"dp": (d + step) % 8, "mp": me},
        )

    def to_partner(step):
        ref = columns((d + 8 - step) % 8)
        return remote(ref, ref, s4s.at[step], s4r.at[step], partner)

    def send_rest(begin, end):
        def send(i, carry):
            send_out(EARLY + (chip + i) % (CHUNKS - EARLY))
            return carry

        lax.fori_loop(begin, end, send, 0)

    def sum_up():
        for step in range(1, PIECES):
            scatter(step).start()
        send_rest(0, FIRST)
        total = mine[place]
        for step in range(1, PIECES):
            scatter(step).wait_recv()
            total += got[step]
        own[...] = total
        for step in range(1, CHIPS):
            across_heads(step).start()
        send_rest(FIRST, SECOND)
        heads[chip] = total
        for step in range(1, CHIPS):
            across_heads(step).wait_recv()
        at = pl.multiple_of(place * PIECE, PIECE)
        narrow[:, pl.ds(at, PIECE)] = heads[:, :, 0:PIECE].reshape(QH, PIECE).astype(bf16)
        for step in range(1, 8):
            pieces(step).start()
        to_partner(0).start()
        send_rest(SECOND, CHUNKS - EARLY)
        lines = heads[:, :, PIECE:PACK].reshape(QH, L)
        lines = jnp.concatenate([lines, jnp.zeros_like(lines)], axis=0).T
        rows_out[...] = lines[0:8, :]
        loss_out[0, 0] = jnp.sum(lines[3:4, :])
        for step in range(1, 8):
            pieces(step).wait_recv()
            to_partner(step).start()
        for step in range(8):
            to_partner(step).wait_recv()
        for step in range(1, PIECES):
            scatter(step).wait_send()
        for step in range(1, CHIPS):
            across_heads(step).wait_send()
        for step in range(1, 8):
            pieces(step).wait_send()
        for step in range(8):
            to_partner(step).wait_send()

    hop2(0, KT[0])
    hop2(1, KT[1])
    hop3(0, KT[0])

    def phase(i, carry):
        in_turn(hop3, i + 1)
        in_turn(hop2, i + 2)
        in_turn(hop1, i + FAR)

        @pl.when(i == 0)
        def _():
            for c in w_copies[1:]:
                c.wait()
            for c in w_remote:
                c.wait_recv()

        in_turn(arrived, i)

        @pl.when(i >= CHUNKS - EARLY // 2)
        def _():
            for n in range(2):
                send_out((i - (CHUNKS - EARLY // 2)) * 2 + (chip + n) % 2)

        compute(i)
        return carry

    lax.fori_loop(0, CHUNKS, phase, 0)

    packed = jnp.zeros((RATIO, L), f32)
    for n in range(4):
        line = jnp.sum(small[n * RATIO : (n + 1) * RATIO, :], axis=1, keepdims=True)
        packed = jnp.where(col_i[:RATIO] == n, line, packed)
    for r in range(PIECES):
        cols = slice(r * PIECE, (r + 1) * PIECE)
        mine[r, :, 0:PIECE] = gw[0:8, cols] + gw[8:16, cols]
        mine[r, :, PIECE:PACK] = packed
    sum_up()

    def finish(i, carry):
        in_turn(all_sent, i)
        exchange(i).wait_send()
        target, far, _ = out_copy(i)
        pl.when(target != me)(lambda: far().wait_send())
        dst = out.at[:, pl.ds(pl.multiple_of(i * KB, KB), KB)]
        pltpu.make_async_copy(mixed.at[i], dst, o_rs.at[i]).wait()
        return carry

    lax.fori_loop(0, CHUNKS, finish, 0)
    for c in w_remote:
        c.wait_send()


def fused(order, bias, decay, gain, positions, hidden, qw, kvw, dtw):
    smem = pl.BlockSpec(memory_space=pltpu.SMEM)
    vmem = pl.BlockSpec(memory_space=pltpu.VMEM)
    hbm = pl.BlockSpec(memory_space=pl.ANY)
    dma = pltpu.SemaphoreType.DMA
    stacked = (RATIO * L, HD)
    return pl.pallas_call(
        body,
        out_shape=(
            jax.ShapeDtypeStruct((L, D), bf16),
            jax.ShapeDtypeStruct((QH, D), bf16),
            jax.ShapeDtypeStruct((8, L), f32),
            jax.ShapeDtypeStruct((1, 1), f32),
        ),
        in_specs=[smem, smem, smem, smem, vmem, vmem, hbm, hbm, hbm],
        out_specs=(hbm, vmem, vmem, smem),
        scratch_shapes=[
            pltpu.VMEM((PIECES, RATIO, PACK), f32),
            pltpu.VMEM((CHUNKS, CHIPS, L, KB), bf16),
            pltpu.VMEM((D, NW), bf16),
            pltpu.VMEM((CHUNKS, L, 512), bf16),
            pltpu.VMEM((RATIO, D), f32),
            pltpu.VMEM((32, D), bf16),
            pltpu.VMEM((L, NW), f32),
            pltpu.VMEM(stacked, bf16),
            pltpu.VMEM(stacked, bf16),
            pltpu.VMEM(stacked, f32),
            pltpu.VMEM(stacked, f32),
            pltpu.VMEM(stacked, f32),
            pltpu.VMEM(stacked, bf16),
            pltpu.VMEM((RATIO * L, 2 * HD), f32),
            pltpu.VMEM((16, D), f32),
            pltpu.VMEM((32, L), f32),
            pltpu.VMEM((CHUNKS, L, KB), bf16),
            dma((CHUNKS,)),
            dma((CHUNKS,)),
            dma((CHUNKS, 12)),
            dma((CHUNKS, 12)),
            dma((3,)),
            dma((2,)),
            dma((2,)),
            dma((CHUNKS,)),
            dma((CHIPS,)),
            pltpu.VMEM((PIECES, RATIO, PACK), f32),
            pltpu.VMEM((RATIO, PACK), f32),
            pltpu.VMEM((CHIPS, RATIO, PACK), f32),
            dma((PIECES,)),
            dma((PIECES,)),
            dma((CHIPS,)),
            dma((CHIPS,)),
            dma((8,)),
            dma((8,)),
            dma((8,)),
            dma((8,)),
        ],
        name="fused",
        compiler_params=pltpu.CompilerParams(
            collective_id=0, has_side_effects=True, vmem_limit_bytes=60 * 2**20
        ),
    )(order, bias, decay, gain, positions, hidden, qw, kvw, dtw)


def local(
    hidden_in,
    positions,
    assignment,
    query_weight,
    kv_weight,
    dt_weight,
    dt_bias,
    decay_log,
    skip_gain,
):
    student_out, narrow, rows, loss = fused(
        assignment,
        dt_bias,
        decay_log,
        skip_gain,
        positions.reshape(16, L),
        hidden_in.reshape(16, L, 512),
        query_weight,
        kv_weight,
        dt_weight.T,
    )
    grad = narrow.astype(f32)
    return student_out, grad.T, rows[0, :QH], rows[1, :QH], rows[2, :QH], loss.reshape(())


def solution(mesh):
    placed = (
        P("dp", "mp"),
        P("dp"),
        P("dp", None),
        P(None, "mp"),
        P(None, "mp"),
        P(),
        P(),
        P(),
        P(),
    )
    return jax.shard_map(
        local,
        mesh=mesh,
        in_specs=placed,
        out_specs=(P(("dp", "mp"), None), P(), P(), P(), P(), P()),
        check_vma=False,
    )
```
